512 devices in a mesh: along: 32 (over x_lo, z), cross: 16 (over x_hi, y, core).
Axes of the slice: x: 4 (x_hi: 2, x_lo: 2; x = x_hi * 2 + x_lo), y: 4, z: 16, core: 2. Of those that a mesh axis runs over, the one named last changes fastest.
Arguments:
- interface_bins: int32 [2, 7, 512, 2048], P(None, None, 'along', 'cross'), may hold values from 1 to 63
- layer_count: int32 [2, 512, 2048], P(None, 'along', 'cross'), may hold values from 1 to 8
- layer_values: bfloat16 [2, 8, 512, 2048], P(None, None, 'along', 'cross'), may hold values from -6 to 6
- footprint: bfloat16 [33, 33], replicated, may hold values from -0.1875 to 0.1875
- depth_gate: bfloat16 [64, 30], replicated, may hold values from -0.75 to 0.75
Outputs:
- gate_response: float32 [2, 30, 512, 2048], P(None, None, 'along', 'cross')
The draws below stay inside these ranges and needn't reach their ends.
All inputs are finite; a program needn't handle non-finite values.
Results may differ from the reference program's by a relative error of at most 0.0032.
Values may be sent and summed in bfloat16 or wider, within the bound.
No kernel may reach another device: no remote copies, remote signals or barrier semaphores. Data moves between devices by JAX's collectives and lax.ppermute only.
A program may use at most 128 MiB of HBM per device.

```python
import jax
import jax.numpy as jnp
from jax import lax

SAMPLES = 2
BINS = 64
GATES = 30
LAYERS = 8
RADIUS = 16
FOOT = 33
GX = 512
GY = 2048


def with_ends(entries, rng, low, largest):
    shape = entries.shape
    spot = [jax.random.randint(jax.random.fold_in(rng, axis), (), 0, shape[axis]) for axis in range(len(shape))]
    entries = entries.at[tuple(spot)].set(low)
    longest = shape.index(max(shape))
    spot[longest] = (spot[longest] + 1) % shape[longest]
    return entries.at[tuple(spot)].set(largest)


def block_scale(key, extent, pieces, low, high):
    factor_of = 1.0
    for axis_at, shards_of in pieces:
        draws = jax.random.uniform(jax.random.fold_in(jax.random.fold_in(key, 6), axis_at), (shards_of,), jnp.float32, low / len(pieces), high / len(pieces))
        factor_of = factor_of * jnp.repeat(jnp.exp(draws), extent[axis_at] // shards_of).reshape((-1,) + (1,) * (len(extent) - 1 - axis_at))
    return factor_of


def bell_draw(own_key, dims, spread, reach, shards=(), kind=jnp.bfloat16):
    gain = block_scale(own_key, dims, shards, -0.22, 0.18) if shards else 1.0
    array = jax.random.normal(own_key, dims, jnp.float32) * spread * gain
    return jnp.minimum(jnp.maximum(array, -reach), reach).astype(kind)


def setup_inputs(seed: int = 0) -> dict:
    key_of = jax.random.split(jax.random.key(seed), 6)
    return {
        "interface_bins": with_ends(jax.random.randint(key_of[0], (SAMPLES, LAYERS - 1, GX, GY), 1, BINS), jax.random.fold_in(key_of[0], 1), 1, BINS - 1).astype(jnp.int32),
        "layer_count": with_ends(jax.random.randint(key_of[1], (SAMPLES, GX, GY), 1, LAYERS + 1), jax.random.fold_in(key_of[1], 1), 1, LAYERS).astype(jnp.int32),
        "layer_values": bell_draw(key_of[2], (SAMPLES, LAYERS, GX, GY), 1.0, 6.0, ((2, 32), (3, 16))),
        "footprint": bell_draw(key_of[3], (FOOT, FOOT), (FOOT * FOOT) ** -0.5, 0.1875),
        "depth_gate": bell_draw(key_of[4], (BINS, GATES), BINS ** -0.5, 0.75),
    }


def render_one(bounds, count, values):
    level = lax.broadcasted_iota(jnp.int32, (BINS, 1, 1), 0)
    index = jnp.zeros((BINS,) + count.shape, jnp.int32)
    for layer in range(bounds.shape[0]):
        active = (layer < count - 1)[None]
        index = index + jnp.where(active & (bounds[layer][None] <= level), 1, 0).astype(jnp.int32)
    conductivity = jnp.zeros((BINS,) + count.shape, jnp.float32)
    for layer in range(values.shape[0]):
        conductivity = conductivity + jnp.where(index == layer, values[layer][None].astype(jnp.float32), jnp.float32(0.0))
    return conductivity.astype(jnp.bfloat16)


def one_sample(args, footprint, depth_gate):
    bounds, count, values = args
    conductivity = render_one(bounds, count, values).astype(jnp.float32)
    kernel = footprint.astype(jnp.float32)[None, None]
    smoothed = lax.conv_general_dilated(conductivity[:, None], kernel, (1, 1), [(RADIUS, RADIUS), (RADIUS, RADIUS)], precision=lax.Precision.HIGHEST)[:, 0]
    smoothed = smoothed.astype(jnp.bfloat16).astype(jnp.float32)
    return jnp.einsum("bg,bxy->gxy", depth_gate.astype(jnp.float32), smoothed, precision=lax.Precision.HIGHEST)


def reference(interface_bins, layer_count, layer_values, footprint, depth_gate):
    return lax.map(lambda args: one_sample(args, footprint, depth_gate), (interface_bins, layer_count, layer_values))
```

```python
import functools

import jax
import jax.numpy as jnp
from jax import lax
from jax.experimental import pallas as pl
from jax.experimental.pallas import tpu as pltpu
from jax.sharding import PartitionSpec as P

ROWS = 8
COLS = 16
LANES = 128
BINS = 64
LIMIT = 40 * 1024 * 1024
BF16 = jnp.bfloat16
F32 = jnp.float32

NETWORK = (
    (0, 6), (2, 3), (4, 5),
    (0, 2), (1, 4), (3, 6),
    (0, 1), (2, 5), (3, 4),
    (1, 2), (4, 6),
    (2, 3), (4, 5),
    (1, 2), (3, 4), (5, 6),
)


def lane_group(shape):
    return lax.broadcasted_iota(jnp.int32, shape, len(shape) - 1) // COLS


def swap_groups(parts):
    count = len(parts)
    group = lane_group(parts[0].shape)
    rolled = [pltpu.roll(part, COLS * r, 1) if r else part for r, part in enumerate(parts)]
    current = [rolled[(-m) % count] for m in range(count)]
    step = 1
    while step < count:
        chosen = (group // step) % 2 == 1
        current = [jnp.where(chosen, current[(m - step) % count], current[m]) for m in range(count)]
        step *= 2
    return [
        pltpu.roll(part, (LANES - COLS * k) % LANES, 1) if k else part
        for k, part in enumerate(current)
    ]


def pack_kernel(bounds_ref, count_ref, values_ref, raw_ref, plane_ref):
    samples, layers = values_ref.shape[:2]
    rows = count_ref.shape[1]
    channels = 2 * layers
    for s in range(samples):
        count = count_ref[s]
        keys = [
            jnp.where(k < count - 1, bounds_ref[s, k], BINS).astype(F32) for k in range(layers - 1)
        ]
        for low, high in NETWORK:
            keys[low], keys[high] = (
                jnp.minimum(keys[low], keys[high]),
                jnp.maximum(keys[low], keys[high]),
            )
        planes = keys + [jnp.zeros_like(keys[0])]
        planes += [values_ref[s, k].astype(F32) for k in range(layers)]
        for k, plane in enumerate(planes):
            first = (s * channels + k) * rows
            plane_ref[first : first + rows, :] = plane
    for s in range(samples):
        for q in range(rows // ROWS):
            parts = []
            for r in range(ROWS):
                first = s * channels * rows + q * ROWS + r
                parts.append(plane_ref[pl.ds(first, channels, stride=rows), :])
            for k, block in enumerate(swap_groups(parts)):
                raw_ref[k, q, s * channels : (s + 1) * channels, :] = block.astype(BF16)


def render(raw, store):
    channels = raw.shape[0] // 2
    layers = channels // 2
    level = lax.broadcasted_iota(jnp.int32, (BINS, LANES), 0).astype(F32).astype(BF16)
    wide = raw.astype(F32)
    for s in range(2):

        def row(k):
            line = wide[s * channels + k : s * channels + k + 1, :]
            line = jnp.broadcast_to(line, (16, LANES)).astype(BF16)
            return jnp.concatenate([line] * (BINS // 16), axis=0)

        bins = row(layers)
        for k in range(layers - 1):
            bins = jnp.where(row(k) <= level, row(layers + 1 + k), bins)
        store(s, bins)


def weights(footprint_ref, taps_ref, fan_ref, turned_ref, bands_ref):
    side = footprint_ref.shape[0]
    taps_ref[...] = jnp.zeros_like(taps_ref)
    taps_ref[ROWS : ROWS + side, :side] = footprint_ref[...].astype(F32)
    shape = (LANES, 3 * LANES)
    dy = lax.broadcasted_iota(jnp.int32, shape, 0)
    lane = lax.broadcasted_iota(jnp.int32, shape, 1)
    pick = (dy == COLS * (lane // LANES) - lane % COLS).astype(F32).astype(BF16)
    fan_ref[...] = jnp.dot(taps_ref[...].astype(BF16), pick, preferred_element_type=F32)
    depth = turned_ref.shape[0]
    group = lane_group((depth, LANES))
    for e in range(3):
        lanes = slice(e * LANES, (e + 1) * LANES)
        turned = jnp.zeros((depth, LANES), F32)
        for r in range(ROWS):
            turned = jnp.where(group == r, fan_ref[ROWS - r : ROWS - r + depth, lanes], turned)
        turned_ref[:, lanes] = turned
    shape = (COLS, LANES)
    later = lax.broadcasted_iota(jnp.int32, shape, 1) % COLS >= lax.broadcasted_iota(
        jnp.int32, shape, 0
    )
    nothing = jnp.zeros((LANES, LANES), BF16)
    for dq in range(depth // ROWS):
        bands_ref[dq, 0, :, LANES:] = nothing
        bands_ref[dq, 3, :, :LANES] = nothing
        for r in range(ROWS):
            at = dq * ROWS + r
            lines = [
                jnp.broadcast_to(turned_ref[at : at + 1, e * LANES : (e + 1) * LANES], shape)
                for e in range(3)
            ]
            same = [pltpu.roll(line, 0, 1, stride=1, stride_axis=0) for line in lines]
            next_ = [
                pltpu.roll(line, LANES - COLS, 1, stride=1, stride_axis=0) for line in lines[1:]
            ]
            next_.append(jnp.zeros(shape, F32))
            for e in range(3):
                block = jnp.where(later, same[e], next_[e]).astype(BF16)
                span = slice(r * COLS, (r + 1) * COLS)
                bands_ref[dq, e, span, :LANES] = block
                bands_ref[dq, e + 1, span, LANES:] = block


def own_kernel(
    raw_ref, footprint_ref, gates_ref, own_ref, bands_ref, mix_ref, taps_ref, fan_ref, turned_ref, mixed_ref
):
    weights(footprint_ref, taps_ref, fan_ref, turned_ref, bands_ref)
    gates, bins = gates_ref.shape
    half = mix_ref.shape[0] // 2
    mixed_ref[...] = jnp.zeros_like(mixed_ref)
    for s in range(2):
        mixed_ref[s * half : s * half + gates, s * bins : (s + 1) * bins] = gates_ref[...].astype(F32)
    mix_ref[...] = mixed_ref[...].astype(BF16)
    blocks, groups = raw_ref.shape[:2]

    @pl.loop(0, blocks)
    def _(k):
        for q in range(groups):

            def store(s, block):
                own_ref[k, q, s * BINS : (s + 1) * BINS, :] = block

            render(raw_ref[k, q], store)


def edge_kernel(before_ref, raw_ref, after_ref, last_ref, first_ref):
    groups = raw_ref.shape[1]
    for target, k in ((last_ref, raw_ref.shape[0] - 1), (first_ref, 0)):
        for at, source in enumerate((before_ref, raw_ref, after_ref)):
            target[at * groups : (at + 1) * groups] = source[k]


def middle_kernel(
    before_ref, own_ref, after_ref, bands_ref, mix_ref, part_ref, mid_ref, around_ref
):
    blocks, groups = before_ref.shape[:2]
    for at, source in enumerate((before_ref, after_ref)):

        @pl.loop(0, blocks)
        def _(k):
            for q in range(groups):

                def store(s, block):
                    around_ref[at, k, q, s * BINS : (s + 1) * BINS, :] = block

                render(source[k, q], store)

    def piece(k, q):
        if q < groups:
            return around_ref[0, k, q]
        if q < 2 * groups:
            return own_ref[k, q - groups]
        return around_ref[1, k, q - 2 * groups]

    reach = bands_ref.shape[0]
    pairs = blocks // 2
    for pair in range(pairs):
        inner = [j for j in range(4) if 0 <= 2 * pair + j - 1 < blocks]
        total = None
        for dq in range(reach):
            left = jnp.concatenate(
                [
                    jnp.concatenate([piece(2 * pair + j - 1, a + dq) for j in inner], axis=1)
                    for a in range(groups)
                ],
                axis=0,
            )
            right = bands_ref[dq, inner[0] : inner[-1] + 1].reshape(len(inner) * LANES, 2 * LANES)
            term = jnp.dot(left, right, preferred_element_type=F32)
            total = term if total is None else total + term
        depth = total.shape[0] // groups
        for side in range(2):
            block = 2 * pair + side
            lanes = slice(side * LANES, (side + 1) * LANES)
            if block == 0:
                part_ref[0] = total[:, lanes]
            elif block == blocks - 1:
                part_ref[1] = total[:, lanes]
            else:
                for a in range(groups):
                    smooth = total[a * depth : (a + 1) * depth, lanes].astype(BF16)
                    mid_ref[a, block - 1] = jnp.dot(
                        mix_ref[...], smooth, preferred_element_type=F32
                    )


def finish_kernel(left_ref, right_ref, bands_ref, mix_ref, part_ref, mid_ref, out_ref, halo_ref):
    spans = left_ref.shape[0]
    groups, mids = mid_ref.shape[:2]
    reach = bands_ref.shape[0]

    @pl.loop(0, spans)
    def _(q):
        for at, source in enumerate((left_ref, right_ref)):

            def store(s, block):
                halo_ref[at, q, s * BINS : (s + 1) * BINS, :] = block

            render(source[q], store)

    ends = []
    for at, (j, lanes) in enumerate(((0, slice(0, LANES)), (3, slice(LANES, 2 * LANES)))):
        left = jnp.concatenate(
            [
                jnp.concatenate([halo_ref[at, a + dq] for dq in range(reach)], axis=1)
                for a in range(groups)
            ],
            axis=0,
        )
        right = jnp.concatenate([bands_ref[dq, j, :, lanes] for dq in range(reach)], axis=0)
        total = part_ref[at] + jnp.dot(left, right, preferred_element_type=F32)
        depth = total.shape[0] // groups
        ends.append(
            [
                jnp.dot(
                    mix_ref[...],
                    total[a * depth : (a + 1) * depth].astype(BF16),
                    preferred_element_type=F32,
                )
                for a in range(groups)
            ]
        )
    half = mix_ref.shape[0] // 2
    rows = groups * ROWS
    gates = out_ref.shape[0] // (2 * rows)
    for a in range(groups):
        for s in range(2):
            span = slice(s * half, (s + 1) * half)
            parts = [ends[0][a][span]]
            parts += [mid_ref[a, k, span, :] for k in range(mids)]
            parts += [ends[1][a][span]]
            for r, block in enumerate(swap_groups(parts)):
                first = s * gates * rows + a * ROWS + r
                out_ref[pl.ds(first, gates, stride=rows), :] = block[:gates]


def vmem(*shape, dtype=BF16):
    return pltpu.VMEM(shape, dtype)


def near(*arrays):
    return [pltpu.with_memory_space_constraint(array, pltpu.VMEM) for array in arrays]


def call(kernel, out, scratch, args, flops=0, moved=0):
    whole = pl.BlockSpec(memory_space=pltpu.VMEM)
    many = isinstance(out, (list, tuple))
    return pl.pallas_call(
        kernel,
        out_shape=out,
        in_specs=[whole] * len(args),
        out_specs=[whole] * len(out) if many else whole,
        scratch_shapes=scratch,
        compiler_params=pltpu.CompilerParams(vmem_limit_bytes=LIMIT),
        cost_estimate=pl.CostEstimate(flops=flops, bytes_accessed=moved, transcendentals=0),
    )(*args)


def shifted(array, axis, ahead):
    count = lax.axis_size(axis)
    pairs = [(i, i + 1) if ahead else (i + 1, i) for i in range(count - 1)]
    return lax.ppermute(array, axis, pairs)


def local(interface_bins, layer_count, layer_values, footprint, depth_gate):
    samples, layers, rows, width = layer_values.shape
    gates = depth_gate.shape[1]
    blocks, groups, channels = width // COLS, rows // ROWS, 2 * layers * samples
    reach = (footprint.shape[0] + ROWS - 1) // ROWS
    deep = samples * BINS

    raw = call(
        pack_kernel,
        vmem(blocks, groups, channels, LANES),
        [vmem(channels * rows, width, dtype=F32)],
        (interface_bins, layer_count, layer_values),
    )
    before = shifted(raw, "along", True)
    after = shifted(raw, "along", False)
    own, bands, mix = call(
        own_kernel,
        [
            vmem(blocks, groups, deep, LANES),
            vmem(reach, 4, LANES, 2 * LANES),
            vmem(64, deep),
        ],
        [
            vmem(64, LANES, dtype=F32),
            vmem(64, 3 * LANES, dtype=F32),
            vmem(reach * ROWS, 3 * LANES, dtype=F32),
            vmem(64, deep, dtype=F32),
        ],
        (*near(raw), footprint, depth_gate.T),
        flops=2_000_000_000,
        moved=4_000_000,
    )
    last, first = call(
        edge_kernel,
        [vmem(3 * groups, channels, LANES)] * 2,
        [],
        near(before, raw, after),
    )
    left = shifted(last, "cross", True)
    right = shifted(first, "cross", False)
    part, mid = call(
        middle_kernel,
        [
            vmem(2, groups * deep, LANES, dtype=F32),
            vmem(groups, blocks - 2, 64, LANES, dtype=F32),
        ],
        [vmem(2, blocks, groups, deep, LANES)],
        near(before, own, after, bands, mix),
        flops=3_000_000_000,
        moved=4_000_000,
    )
    out = call(
        finish_kernel,
        jax.ShapeDtypeStruct((samples * gates * rows, width), F32),
        [vmem(2, 3 * groups, deep, LANES)],
        near(left, right, bands, mix, part, mid),
    )
    return out.reshape(samples, gates, rows, width)


def solution(mesh):
    in_specs = (
        P(None, None, "along", "cross"),
        P(None, "along", "cross"),
        P(None, None, "along", "cross"),
        P(),
        P(),
    )
    out_specs = P(None, None, "along", "cross")
    return jax.shard_map(local, mesh=mesh, in_specs=in_specs, out_specs=out_specs, check_vma=False)
```

```python
import functools

import jax
import jax.numpy as jnp
from jax import lax
from jax.experimental import pallas as pl
from jax.experimental.pallas import tpu as pltpu
from jax.sharding import PartitionSpec as P

ROWS = 8
COLS = 16
LANES = 128
BINS = 64
LIMIT = 40 * 1024 * 1024
BF16 = jnp.bfloat16
F32 = jnp.float32

NETWORK = (
    (0, 6), (2, 3), (4, 5),
    (0, 2), (1, 4), (3, 6),
    (0, 1), (2, 5), (3, 4),
    (1, 2), (4, 6),
    (2, 3), (4, 5),
    (1, 2), (3, 4), (5, 6),
)


def lane_group(shape):
    return lax.broadcasted_iota(jnp.int32, shape, len(shape) - 1) // COLS


def swap_groups(parts):
    count = len(parts)
    group = lane_group(parts[0].shape)
    rolled = [pltpu.roll(part, COLS * r, 1) if r else part for r, part in enumerate(parts)]
    current = [rolled[(-m) % count] for m in range(count)]
    step = 1
    while step < count:
        chosen = (group // step) % 2 == 1
        current = [jnp.where(chosen, current[(m - step) % count], current[m]) for m in range(count)]
        step *= 2
    return [
        pltpu.roll(part, (LANES - COLS * k) % LANES, 1) if k else part
        for k, part in enumerate(current)
    ]


def fetch(sources, targets, sems):
    copies = [
        pltpu.make_async_copy(source, target, sems.at[at])
        for at, (source, target) in enumerate(zip(sources, targets))
    ]
    for copy in copies:
        copy.start()
    return copies


def pack_kernel(
    bounds_hbm, count_hbm, values_hbm, raw_ref, plane_ref, bounds_ref, count_ref, values_ref, sems
):
    for copy in fetch(
        (bounds_hbm, count_hbm, values_hbm), (bounds_ref, count_ref, values_ref), sems
    ):
        copy.wait()
    samples, layers = values_ref.shape[:2]
    rows = count_ref.shape[1]
    channels = 2 * layers
    for s in range(samples):
        count = count_ref[s]
        keys = [
            jnp.where(k < count - 1, bounds_ref[s, k], BINS).astype(F32) for k in range(layers - 1)
        ]
        for low, high in NETWORK:
            keys[low], keys[high] = (
                jnp.minimum(keys[low], keys[high]),
                jnp.maximum(keys[low], keys[high]),
            )
        planes = keys + [jnp.zeros_like(keys[0])]
        planes += [values_ref[s, k].astype(F32) for k in range(layers)]
        for k, plane in enumerate(planes):
            first = (s * channels + k) * rows
            plane_ref[first : first + rows, :] = plane
    for s in range(samples):
        for q in range(rows // ROWS):
            parts = []
            for r in range(ROWS):
                first = s * channels * rows + q * ROWS + r
                parts.append(plane_ref[pl.ds(first, channels, stride=rows), :])
            for k, block in enumerate(swap_groups(parts)):
                raw_ref[k, q, s * channels : (s + 1) * channels, :] = block.astype(BF16)


def render(raw, store):
    channels = raw.shape[0] // 2
    layers = channels // 2
    level = lax.broadcasted_iota(jnp.int32, (BINS, LANES), 0).astype(F32).astype(BF16)
    wide = raw.astype(F32)
    for s in range(2):

        def row(k):
            line = wide[s * channels + k : s * channels + k + 1, :]
            line = jnp.broadcast_to(line, (16, LANES)).astype(BF16)
            return jnp.concatenate([line] * (BINS // 16), axis=0)

        bins = row(layers)
        for k in range(layers - 1):
            bins = jnp.where(row(k) <= level, row(layers + 1 + k), bins)
        store(s, bins)


def weights(footprint_ref, taps_ref, fan_ref, turned_ref, bands_ref):
    side = footprint_ref.shape[0]
    taps_ref[...] = jnp.zeros_like(taps_ref)
    taps_ref[ROWS : ROWS + side, :side] = footprint_ref[...].astype(F32)
    shape = (LANES, 3 * LANES)
    dy = lax.broadcasted_iota(jnp.int32, shape, 0)
    lane = lax.broadcasted_iota(jnp.int32, shape, 1)
    pick = (dy == COLS * (lane // LANES) - lane % COLS).astype(F32).astype(BF16)
    fan_ref[...] = jnp.dot(taps_ref[...].astype(BF16), pick, preferred_element_type=F32)
    depth = turned_ref.shape[0]
    group = lane_group((depth, LANES))
    for e in range(3):
        lanes = slice(e * LANES, (e + 1) * LANES)
        turned = jnp.zeros((depth, LANES), F32)
        for r in range(ROWS):
            turned = jnp.where(group == r, fan_ref[ROWS - r : ROWS - r + depth, lanes], turned)
        turned_ref[:, lanes] = turned
    shape = (COLS, LANES)
    later = lax.broadcasted_iota(jnp.int32, shape, 1) % COLS >= lax.broadcasted_iota(
        jnp.int32, shape, 0
    )
    nothing = jnp.zeros((LANES, LANES), BF16)
    for dq in range(depth // ROWS):
        bands_ref[dq, 0, :, LANES:] = nothing
        bands_ref[dq, 3, :, :LANES] = nothing
        for r in range(ROWS):
            at = dq * ROWS + r
            lines = [
                jnp.broadcast_to(turned_ref[at : at + 1, e * LANES : (e + 1) * LANES], shape)
                for e in range(3)
            ]
            same = [pltpu.roll(line, 0, 1, stride=1, stride_axis=0) for line in lines]
            next_ = [
                pltpu.roll(line, LANES - COLS, 1, stride=1, stride_axis=0) for line in lines[1:]
            ]
            next_.append(jnp.zeros(shape, F32))
            for e in range(3):
                block = jnp.where(later, same[e], next_[e]).astype(BF16)
                span = slice(r * COLS, (r + 1) * COLS)
                bands_ref[dq, e, span, :LANES] = block
                bands_ref[dq, e + 1, span, LANES:] = block


def own_kernel(
    raw_ref,
    footprint_hbm,
    gates_hbm,
    own_ref,
    bands_ref,
    mix_ref,
    taps_ref,
    fan_ref,
    turned_ref,
    mixed_ref,
    footprint_ref,
    gates_ref,
    sems,
):
    copies = fetch((footprint_hbm, gates_hbm), (footprint_ref, gates_ref), sems)
    blocks, groups = raw_ref.shape[:2]

    @pl.loop(0, blocks)
    def _(k):
        for q in range(groups):

            def store(s, block):
                own_ref[k, q, s * BINS : (s + 1) * BINS, :] = block

            render(raw_ref[k, q], store)

    for copy in copies:
        copy.wait()
    weights(footprint_ref, taps_ref, fan_ref, turned_ref, bands_ref)
    gates, bins = gates_ref.shape
    half = mix_ref.shape[0] // 2
    mixed_ref[...] = jnp.zeros_like(mixed_ref)
    for s in range(2):
        mixed_ref[s * half : s * half + gates, s * bins : (s + 1) * bins] = gates_ref[...].astype(F32)
    mix_ref[...] = mixed_ref[...].astype(BF16)


def parity():
    return lax.rem(lax.axis_index("cross"), 2)


def edge_kernel(after_ref, raw_ref, before_ref, outer_ref, inner_ref):
    groups = raw_ref.shape[1]
    end = raw_ref.shape[0] - 1
    for target, k in ((outer_ref, end * parity()), (inner_ref, end * (1 - parity()))):
        for at, source in enumerate((before_ref, raw_ref, after_ref)):
            target[at * groups : (at + 1) * groups] = source[k]


def middle_kernel(
    after_ref, own_ref, before_ref, bands_ref, mix_ref, part_ref, mid_ref, around_ref
):
    blocks, groups = before_ref.shape[:2]
    for at, source in enumerate((before_ref, after_ref)):

        @pl.loop(0, blocks)
        def _(k):
            for q in range(groups):

                def store(s, block):
                    around_ref[at, k, q, s * BINS : (s + 1) * BINS, :] = block

                render(source[k, q], store)

    def piece(k, q):
        if q < groups:
            return around_ref[0, k, q]
        if q < 2 * groups:
            return own_ref[k, q - groups]
        return around_ref[1, k, q - 2 * groups]

    reach = bands_ref.shape[0]
    pairs = blocks // 2
    for pair in range(pairs):
        inner = [j for j in range(4) if 0 <= 2 * pair + j - 1 < blocks]
        total = None
        for dq in range(reach):
            left = jnp.concatenate(
                [
                    jnp.concatenate([piece(2 * pair + j - 1, a + dq) for j in inner], axis=1)
                    for a in range(groups)
                ],
                axis=0,
            )
            right = bands_ref[dq, inner[0] : inner[-1] + 1].reshape(len(inner) * LANES, 2 * LANES)
            term = jnp.dot(left, right, preferred_element_type=F32)
            total = term if total is None else total + term
        depth = total.shape[0] // groups
        for side in range(2):
            block = 2 * pair + side
            lanes = slice(side * LANES, (side + 1) * LANES)
            if block == 0:
                part_ref[0] = total[:, lanes]
            elif block == blocks - 1:
                part_ref[1] = total[:, lanes]
            else:
                for a in range(groups):
                    smooth = total[a * depth : (a + 1) * depth, lanes].astype(BF16)
                    mid_ref[a, block - 1] = jnp.dot(
                        mix_ref[...], smooth, preferred_element_type=F32
                    )


def finish_kernel(outer_ref, inner_ref, bands_ref, mix_ref, part_ref, mid_ref, out_ref, halo_ref):
    spans = outer_ref.shape[0]
    groups, mids = mid_ref.shape[:2]
    reach = bands_ref.shape[0]

    @pl.loop(0, spans)
    def _(q):
        for at, source in ((parity(), outer_ref), (1 - parity(), inner_ref)):

            def store(s, block):
                halo_ref[at, q, s * BINS : (s + 1) * BINS, :] = block

            render(source[q], store)

    ends = []
    for at, (j, lanes) in enumerate(((0, slice(0, LANES)), (3, slice(LANES, 2 * LANES)))):
        left = jnp.concatenate(
            [
                jnp.concatenate([halo_ref[at, a + dq] for dq in range(reach)], axis=1)
                for a in range(groups)
            ],
            axis=0,
        )
        right = jnp.concatenate([bands_ref[dq, j, :, lanes] for dq in range(reach)], axis=0)
        total = part_ref[at] + jnp.dot(left, right, preferred_element_type=F32)
        depth = total.shape[0] // groups
        ends.append(
            [
                jnp.dot(
                    mix_ref[...],
                    total[a * depth : (a + 1) * depth].astype(BF16),
                    preferred_element_type=F32,
                )
                for a in range(groups)
            ]
        )
    half = mix_ref.shape[0] // 2
    rows = groups * ROWS
    gates = out_ref.shape[0] // (2 * rows)
    for a in range(groups):
        for s in range(2):
            span = slice(s * half, (s + 1) * half)
            parts = [ends[0][a][span]]
            parts += [mid_ref[a, k, span, :] for k in range(mids)]
            parts += [ends[1][a][span]]
            for r, block in enumerate(swap_groups(parts)):
                first = s * gates * rows + a * ROWS + r
                out_ref[pl.ds(first, gates, stride=rows), :] = block[:gates]


def vmem(*shape, dtype=BF16):
    return pltpu.VMEM(shape, dtype)


def far(*arrays):
    return [pltpu.with_memory_space_constraint(array, pltpu.HBM) for array in arrays]


def near(*arrays):
    return [pltpu.with_memory_space_constraint(array, pltpu.VMEM) for array in arrays]


def call(kernel, out, scratch, args, remote=(), flops=0, moved=0):
    whole = pl.BlockSpec(memory_space=pltpu.VMEM)
    many = isinstance(out, (list, tuple))
    if remote:
        scratch = scratch + [pltpu.VMEM(array.shape, array.dtype) for array in remote]
        scratch.append(pltpu.SemaphoreType.DMA((len(remote),)))
    return pl.pallas_call(
        kernel,
        out_shape=out,
        in_specs=[whole] * len(args) + [pl.BlockSpec(memory_space=pl.ANY)] * len(remote),
        out_specs=[whole] * len(out) if many else whole,
        scratch_shapes=scratch,
        compiler_params=pltpu.CompilerParams(vmem_limit_bytes=LIMIT),
        cost_estimate=pl.CostEstimate(flops=flops, bytes_accessed=moved, transcendentals=0),
    )(*near(*args), *far(*remote))


def shifted(array, axis, ahead):
    count = lax.axis_size(axis)
    pairs = [(i, i + 1) if ahead else (i + 1, i) for i in range(count - 1)]
    return lax.ppermute(array, axis, pairs)


def exchanged(array, axis, first):
    count = lax.axis_size(axis)
    pairs = [(i, i + 1) for i in range(first, count - 1, 2)]
    return lax.ppermute(array, axis, pairs + [(j, i) for i, j in pairs])


def local(interface_bins, layer_count, layer_values, footprint, depth_gate):
    samples, layers, rows, width = layer_values.shape
    gates = depth_gate.shape[1]
    blocks, groups, channels = width // COLS, rows // ROWS, 2 * layers * samples
    reach = (footprint.shape[0] + ROWS - 1) // ROWS
    deep = samples * BINS

    raw = call(
        pack_kernel,
        vmem(blocks, groups, channels, LANES),
        [vmem(channels * rows, width, dtype=F32)],
        (),
        remote=(interface_bins, layer_count, layer_values),
    )
    after = shifted(raw, "along", False)
    before = shifted(raw, "along", True)
    own, bands, mix = call(
        own_kernel,
        [
            vmem(blocks, groups, deep, LANES),
            vmem(reach, 4, LANES, 2 * LANES),
            vmem(64, deep),
        ],
        [
            vmem(64, LANES, dtype=F32),
            vmem(64, 3 * LANES, dtype=F32),
            vmem(reach * ROWS, 3 * LANES, dtype=F32),
            vmem(64, deep, dtype=F32),
        ],
        (raw,),
        remote=(footprint, depth_gate.T),
        flops=2_000_000_000,
        moved=4_000_000,
    )
    outer, inner = call(
        edge_kernel,
        [vmem(3 * groups, channels, LANES)] * 2,
        [],
        (after, raw, before),
    )
    outer = exchanged(outer, "cross", 1)
    inner = exchanged(inner, "cross", 0)
    part, mid = call(
        middle_kernel,
        [
            vmem(2, groups * deep, LANES, dtype=F32),
            vmem(groups, blocks - 2, 64, LANES, dtype=F32),
        ],
        [vmem(2, blocks, groups, deep, LANES)],
        (after, own, before, bands, mix),
        flops=3_000_000_000,
        moved=4_000_000,
    )
    out = call(
        finish_kernel,
        jax.ShapeDtypeStruct((samples * gates * rows, width), F32),
        [vmem(2, 3 * groups, deep, LANES)],
        (outer, inner, bands, mix, part, mid),
    )
    return out.reshape(samples, gates, rows, width)


def solution(mesh):
    in_specs = (
        P(None, None, "along", "cross"),
        P(None, "along", "cross"),
        P(None, None, "along", "cross"),
        P(),
        P(),
    )
    out_specs = P(None, None, "along", "cross")
    return jax.shard_map(local, mesh=mesh, in_specs=in_specs, out_specs=out_specs, check_vma=False)
```

```python
import functools

import jax
import jax.numpy as jnp
from jax import lax
from jax.experimental import pallas as pl
from jax.experimental.pallas import tpu as pltpu
from jax.sharding import PartitionSpec as P

ROWS = 8
COLS = 16
LANES = 128
BINS = 64
LIMIT = 40 * 1024 * 1024
BF16 = jnp.bfloat16
F32 = jnp.float32

NETWORK = (
    (0, 6), (2, 3), (4, 5),
    (0, 2), (1, 4), (3, 6),
    (0, 1), (2, 5), (3, 4),
    (1, 2), (4, 6),
    (2, 3), (4, 5),
    (1, 2), (3, 4), (5, 6),
)


def lane_group(shape):
    return lax.broadcasted_iota(jnp.int32, shape, len(shape) - 1) // COLS


def swap_groups(parts):
    count = len(parts)
    group = lane_group(parts[0].shape)
    rolled = [pltpu.roll(part, COLS * r, 1) if r else part for r, part in enumerate(parts)]
    current = [rolled[(-m) % count] for m in range(count)]
    step = 1
    while step < count:
        chosen = (group // step) % 2 == 1
        current = [jnp.where(chosen, current[(m - step) % count], current[m]) for m in range(count)]
        step *= 2
    return [
        pltpu.roll(part, (LANES - COLS * k) % LANES, 1) if k else part
        for k, part in enumerate(current)
    ]


def fetch(sources, targets, sems):
    copies = [
        pltpu.make_async_copy(source, target, sems.at[at])
        for at, (source, target) in enumerate(zip(sources, targets))
    ]
    for copy in copies:
        copy.start()
    return copies


def pack_kernel(
    bounds_hbm, count_hbm, values_hbm, raw_ref, plane_ref, bounds_ref, count_ref, values_ref, sems
):
    for copy in fetch(
        (bounds_hbm, count_hbm, values_hbm), (bounds_ref, count_ref, values_ref), sems
    ):
        copy.wait()
    samples, layers = values_ref.shape[:2]
    rows = count_ref.shape[1]
    channels = 2 * layers
    for s in range(samples):
        count = count_ref[s]
        keys = [
            jnp.where(k < count - 1, bounds_ref[s, k], BINS).astype(F32) for k in range(layers - 1)
        ]
        for low, high in NETWORK:
            keys[low], keys[high] = (
                jnp.minimum(keys[low], keys[high]),
                jnp.maximum(keys[low], keys[high]),
            )
        planes = keys + [jnp.zeros_like(keys[0])]
        planes += [values_ref[s, k].astype(F32) for k in range(layers)]
        for k, plane in enumerate(planes):
            first = (s * channels + k) * rows
            plane_ref[first : first + rows, :] = plane
    for s in range(samples):
        for q in range(rows // ROWS):
            parts = []
            for r in range(ROWS):
                first = s * channels * rows + q * ROWS + r
                parts.append(plane_ref[pl.ds(first, channels, stride=rows), :])
            for k, block in enumerate(swap_groups(parts)):
                raw_ref[k, q, s * channels : (s + 1) * channels, :] = block.astype(BF16)


def render(raw, store):
    channels = raw.shape[0] // 2
    layers = channels // 2
    level = lax.broadcasted_iota(jnp.int32, (BINS, LANES), 0).astype(F32).astype(BF16)
    wide = raw.astype(F32)
    for s in range(2):

        def row(k):
            line = wide[s * channels + k : s * channels + k + 1, :]
            line = jnp.broadcast_to(line, (16, LANES)).astype(BF16)
            return jnp.concatenate([line] * (BINS // 16), axis=0)

        bins = row(layers)
        for k in range(layers - 1):
            bins = jnp.where(row(k) <= level, row(layers + 1 + k), bins)
        store(s, bins)


def weights(footprint_ref, taps_ref, fan_ref, turned_ref, bands_ref):
    side = footprint_ref.shape[0]
    taps_ref[...] = jnp.zeros_like(taps_ref)
    taps_ref[ROWS : ROWS + side, :side] = footprint_ref[...].astype(F32)
    shape = (LANES, 3 * LANES)
    dy = lax.broadcasted_iota(jnp.int32, shape, 0)
    lane = lax.broadcasted_iota(jnp.int32, shape, 1)
    pick = (dy == COLS * (lane // LANES) - lane % COLS).astype(F32).astype(BF16)
    fan_ref[...] = jnp.dot(taps_ref[...].astype(BF16), pick, preferred_element_type=F32)
    depth = turned_ref.shape[0]
    group = lane_group((depth, LANES))
    for e in range(3):
        lanes = slice(e * LANES, (e + 1) * LANES)
        turned = jnp.zeros((depth, LANES), F32)
        for r in range(ROWS):
            turned = jnp.where(group == r, fan_ref[ROWS - r : ROWS - r + depth, lanes], turned)
        turned_ref[:, lanes] = turned
    shape = (COLS, LANES)
    later = lax.broadcasted_iota(jnp.int32, shape, 1) % COLS >= lax.broadcasted_iota(
        jnp.int32, shape, 0
    )
    nothing = jnp.zeros((LANES, LANES), BF16)
    for e in range(3):
        bands_ref[0, e, :LANES, LANES:] = nothing
        bands_ref[2, e, LANES:, :LANES] = nothing
    for dq in range(depth // ROWS):
        for r in range(ROWS):
            at = dq * ROWS + r
            lines = [
                jnp.broadcast_to(turned_ref[at : at + 1, e * LANES : (e + 1) * LANES], shape)
                for e in range(3)
            ]
            same = [pltpu.roll(line, 0, 1, stride=1, stride_axis=0) for line in lines]
            next_ = [
                pltpu.roll(line, LANES - COLS, 1, stride=1, stride_axis=0) for line in lines[1:]
            ]
            next_.append(jnp.zeros(shape, F32))
            for e in range(3):
                block = jnp.where(later, same[e], next_[e]).astype(BF16)
                for a in range(2):
                    first = (dq + a) % 2 * LANES + r * COLS
                    bands_ref[
                        (dq + a) // 2, e, first : first + COLS, a * LANES : (a + 1) * LANES
                    ] = block


def render_all(raw_ref, bins_ref):
    blocks, groups = raw_ref.shape[:2]

    @pl.loop(0, blocks)
    def _(k):
        for q in range(groups):

            def store(s, block):
                bins_ref[k, s * BINS : (s + 1) * BINS, q * LANES : (q + 1) * LANES] = block

            render(raw_ref[k, q], store)


def own_kernel(
    raw_ref,
    footprint_hbm,
    gates_hbm,
    own_ref,
    bands_ref,
    mix_ref,
    taps_ref,
    fan_ref,
    turned_ref,
    mixed_ref,
    footprint_ref,
    gates_ref,
    sems,
):
    copies = fetch((footprint_hbm, gates_hbm), (footprint_ref, gates_ref), sems)
    render_all(raw_ref, own_ref)
    for copy in copies:
        copy.wait()
    weights(footprint_ref, taps_ref, fan_ref, turned_ref, bands_ref)
    gates, bins = gates_ref.shape
    half = mix_ref.shape[0] // 2
    mixed_ref[...] = jnp.zeros_like(mixed_ref)
    for s in range(2):
        mixed_ref[s * half : s * half + gates, s * bins : (s + 1) * bins] = gates_ref[...].astype(F32)
    mix_ref[...] = mixed_ref[...].astype(BF16)


def parity():
    return lax.rem(lax.axis_index("cross"), 2)


def edge_kernel(after_ref, raw_ref, before_ref, outer_ref, inner_ref):
    groups = raw_ref.shape[1]
    end = raw_ref.shape[0] - 1
    for target, k in ((outer_ref, end * parity()), (inner_ref, end * (1 - parity()))):
        for at, source in enumerate((before_ref, raw_ref, after_ref)):
            target[at * groups : (at + 1) * groups] = source[k]


def around_kernel(
    after_ref, own_ref, before_ref, bands_ref, mix_ref, ends_ref, mid_ref, below_ref, above_ref
):
    render_all(after_ref, below_ref)
    render_all(before_ref, above_ref)
    blocks, deep = own_ref.shape[:2]
    nothing = jnp.zeros(own_ref.shape[1:], BF16)

    def shifted_rows(source, e):
        parts = [source[k] for k in range(max(e - 1, 0), min(blocks + e - 1, blocks))]
        parts = [nothing] * (e == 0) + parts + [nothing] * (e == 2)
        return jnp.concatenate(parts, axis=0)

    left = jnp.concatenate(
        [shifted_rows(source, e) for source in (above_ref, own_ref, below_ref) for e in range(3)],
        axis=1,
    )
    right = bands_ref[...].reshape(9 * 2 * LANES, 2 * LANES)
    total = jnp.dot(left, right, preferred_element_type=F32)
    ends_ref[0] = total[:deep]
    ends_ref[1] = total[(blocks - 1) * deep :]
    smooth = total[deep : (blocks - 1) * deep].astype(BF16)
    for k in range(blocks - 2):
        mid_ref[k] = jnp.dot(
            mix_ref[...], smooth[k * deep : (k + 1) * deep], preferred_element_type=F32
        )


def finish_kernel(
    outer_ref, inner_ref, bands_ref, mix_ref, ends_ref, mid_ref, out_hbm, halo_ref, out_ref, sems
):
    spans = outer_ref.shape[0]
    groups = spans // 3
    for at, source in ((parity(), outer_ref), (1 - parity(), inner_ref)):

        @pl.loop(0, 3)
        def _(t):
            for q in range(groups):

                def store(s, block):
                    halo_ref[at, t, s * BINS : (s + 1) * BINS, q * LANES : (q + 1) * LANES] = block

                render(source[t * groups + q], store)

    mixed = [mid_ref[k] for k in range(mid_ref.shape[0])]
    for at, e in ((0, 0), (1, 2)):
        left = jnp.concatenate([halo_ref[at, t] for t in range(3)], axis=1)
        right = jnp.concatenate([bands_ref[t, e] for t in range(3)], axis=0)
        smooth = ends_ref[at] + jnp.dot(left, right, preferred_element_type=F32)
        block = jnp.dot(mix_ref[...], smooth.astype(BF16), preferred_element_type=F32)
        mixed = [block] + mixed if at == 0 else mixed + [block]
    half = mix_ref.shape[0] // 2
    rows = groups * ROWS
    gates = out_ref.shape[0] // (2 * rows)
    copies = []
    for s in range(2):
        for a in range(groups):
            parts = [
                block[s * half : (s + 1) * half, a * LANES : (a + 1) * LANES] for block in mixed
            ]
            for r, block in enumerate(swap_groups(parts)):
                first = s * gates * rows + a * ROWS + r
                out_ref[pl.ds(first, gates, stride=rows), :] = block[:gates]
        span = pl.ds(s * gates * rows, gates * rows)
        copies.append(pltpu.make_async_copy(out_ref.at[span], out_hbm.at[span], sems.at[s]))
        copies[-1].start()
    for copy in copies:
        copy.wait()


def vmem(*shape, dtype=BF16):
    return pltpu.VMEM(shape, dtype)


def far(*arrays):
    return [pltpu.with_memory_space_constraint(array, pltpu.HBM) for array in arrays]


def near(*arrays):
    return [pltpu.with_memory_space_constraint(array, pltpu.VMEM) for array in arrays]


def call(kernel, out, scratch, args, remote=(), flops=0, moved=0, place=pltpu.VMEM):
    whole = pl.BlockSpec(memory_space=pltpu.VMEM)
    there = pl.BlockSpec(memory_space=place)
    many = isinstance(out, (list, tuple))
    if remote:
        scratch = scratch + [pltpu.VMEM(array.shape, array.dtype) for array in remote]
        scratch.append(pltpu.SemaphoreType.DMA((len(remote),)))
    return pl.pallas_call(
        kernel,
        out_shape=out,
        in_specs=[whole] * len(args) + [pl.BlockSpec(memory_space=pl.ANY)] * len(remote),
        out_specs=[there] * len(out) if many else there,
        scratch_shapes=scratch,
        compiler_params=pltpu.CompilerParams(vmem_limit_bytes=LIMIT),
        cost_estimate=pl.CostEstimate(flops=flops, bytes_accessed=moved, transcendentals=0),
    )(*near(*args), *far(*remote))


def shifted(array, axis, ahead):
    count = lax.axis_size(axis)
    pairs = [(i, i + 1) if ahead else (i + 1, i) for i in range(count - 1)]
    return lax.ppermute(array, axis, pairs)


def exchanged(array, axis, first):
    count = lax.axis_size(axis)
    pairs = [(i, i + 1) for i in range(first, count - 1, 2)]
    return lax.ppermute(array, axis, pairs + [(j, i) for i, j in pairs])


def local(interface_bins, layer_count, layer_values, footprint, depth_gate):
    samples, layers, rows, width = layer_values.shape
    gates = depth_gate.shape[1]
    blocks, groups, channels = width // COLS, rows // ROWS, 2 * layers * samples
    lines = -(-footprint.shape[0] // ROWS) * ROWS
    deep = samples * BINS

    raw = call(
        pack_kernel,
        vmem(blocks, groups, channels, LANES),
        [vmem(channels * rows, width, dtype=F32)],
        (),
        remote=(interface_bins, layer_count, layer_values),
    )
    after = shifted(raw, "along", False)
    before = shifted(raw, "along", True)
    own, bands, mix = call(
        own_kernel,
        [
            vmem(blocks, deep, groups * LANES),
            vmem(3, 3, 2 * LANES, 2 * LANES),
            vmem(64, deep),
        ],
        [
            vmem(64, LANES, dtype=F32),
            vmem(64, 3 * LANES, dtype=F32),
            vmem(lines, 3 * LANES, dtype=F32),
            vmem(64, deep, dtype=F32),
        ],
        (raw,),
        remote=(footprint, depth_gate.T),
        flops=2_000_000_000,
        moved=4_000_000,
    )
    outer, inner = call(
        edge_kernel,
        [vmem(3 * groups, channels, LANES)] * 2,
        [],
        (after, raw, before),
    )
    outer = exchanged(outer, "cross", 1)
    inner = exchanged(inner, "cross", 0)
    ends, mid = call(
        around_kernel,
        [
            vmem(2, deep, groups * LANES, dtype=F32),
            vmem(blocks - 2, 64, groups * LANES, dtype=F32),
        ],
        [vmem(blocks, deep, groups * LANES)] * 2,
        (after, own, before, bands, mix),
        flops=3_000_000_000,
        moved=4_000_000,
    )
    out = call(
        finish_kernel,
        jax.ShapeDtypeStruct((samples * gates * rows, width), F32),
        [
            vmem(2, 3, deep, groups * LANES),
            vmem(samples * gates * rows, width, dtype=F32),
            pltpu.SemaphoreType.DMA((samples,)),
        ],
        (outer, inner, bands, mix, ends, mid),
        place=pl.ANY,
    )
    return out.reshape(samples, gates, rows, width)


def solution(mesh):
    in_specs = (
        P(None, None, "along", "cross"),
        P(None, "along", "cross"),
        P(None, None, "along", "cross"),
        P(),
        P(),
    )
    out_specs = P(None, None, "along", "cross")
    return jax.shard_map(local, mesh=mesh, in_specs=in_specs, out_specs=out_specs, check_vma=False)
```

```python
import functools

import jax
import jax.numpy as jnp
from jax import lax
from jax.experimental import pallas as pl
from jax.experimental.pallas import tpu as pltpu
from jax.sharding import PartitionSpec as P

ROWS = 8
COLS = 16
LANES = 128
BINS = 64
LIMIT = 40 * 1024 * 1024
BF16 = jnp.bfloat16
F32 = jnp.float32

NETWORK = (
    (0, 6), (2, 3), (4, 5),
    (0, 2), (1, 4), (3, 6),
    (0, 1), (2, 5), (3, 4),
    (1, 2), (4, 6),
    (2, 3), (4, 5),
    (1, 2), (3, 4), (5, 6),
)


def lane_group(shape):
    return lax.broadcasted_iota(jnp.int32, shape, len(shape) - 1) // COLS


def staggered(parts, sign):
    count = len(parts)
    group = lane_group(parts[0].shape)
    step = 1
    while step < count:
        chosen = (group // step) % 2 == 1
        parts = [
            jnp.where(chosen, parts[(m + sign * step) % count], parts[m]) for m in range(count)
        ]
        step *= 2
    return parts


def swap_groups(parts):
    count = len(parts)
    parts = [
        pltpu.roll(part, COLS * d, 1) if d else part for d, part in enumerate(staggered(parts, 1))
    ]
    return staggered([parts[-m % count] for m in range(count)], -1)


def pack_kernel(
    bounds_hbm,
    count_hbm,
    values_hbm,
    footprint_hbm,
    gates_hbm,
    raw_ref,
    footprint_ref,
    gates_ref,
    plane_ref,
    bounds_ref,
    count_ref,
    values_ref,
    sems,
):
    samples, layers = values_ref.shape[:2]
    rows = count_ref.shape[1]
    channels = 2 * layers
    copies = []
    for s in range(samples):
        for source, target in (
            (bounds_hbm, bounds_ref), (count_hbm, count_ref), (values_hbm, values_ref)
        ):
            copies.append((source.at[s], target.at[s]))
    copies += [(footprint_hbm, footprint_ref), (gates_hbm, gates_ref)]
    copies = [
        pltpu.make_async_copy(source, target, sems.at[at])
        for at, (source, target) in enumerate(copies)
    ]
    for copy in copies:
        copy.start()
    for s in range(samples):
        for copy in copies[3 * s : 3 * s + 3]:
            copy.wait()
        count = count_ref[s]
        keys = [
            jnp.where(k < count - 1, bounds_ref[s, k], BINS).astype(F32) for k in range(layers - 1)
        ]
        for low, high in NETWORK:
            keys[low], keys[high] = (
                jnp.minimum(keys[low], keys[high]),
                jnp.maximum(keys[low], keys[high]),
            )
        planes = keys + [jnp.zeros_like(keys[0])]
        planes += [values_ref[s, k].astype(F32) for k in range(layers)]
        for k, plane in enumerate(planes):
            first = (s * channels + k) * rows
            plane_ref[first : first + rows, :] = plane
        for q in range(rows // ROWS):
            parts = []
            for r in range(ROWS):
                first = s * channels * rows + q * ROWS + r
                parts.append(plane_ref[pl.ds(first, channels, stride=rows), :])
            for k, block in enumerate(swap_groups(parts)):
                raw_ref[k, q, s * channels : (s + 1) * channels, :] = block.astype(BF16)
    for copy in copies[3 * samples :]:
        copy.wait()


def render(raw):
    channels = raw.shape[0] // 2
    layers = channels // 2
    level = lax.broadcasted_iota(jnp.int32, (BINS, LANES), 0).astype(F32).astype(BF16)
    wide = raw.astype(F32)
    both = []
    for s in range(2):

        def row(k):
            line = wide[s * channels + k : s * channels + k + 1, :]
            line = jnp.broadcast_to(line, (16, LANES)).astype(BF16)
            return jnp.concatenate([line] * (BINS // 16), axis=0)

        bins = row(layers)
        for k in range(layers - 1):
            bins = jnp.where(row(k) <= level, row(layers + 1 + k), bins)
        both.append(bins)
    return jnp.concatenate(both, axis=0)


def weights(footprint_ref, taps_ref, fan_ref, turned_ref, bands_ref):
    side = footprint_ref.shape[0]
    taps_ref[...] = jnp.zeros_like(taps_ref)
    taps_ref[ROWS : ROWS + side, :side] = footprint_ref[...].astype(F32)
    shape = (LANES, 3 * LANES)
    dy = lax.broadcasted_iota(jnp.int32, shape, 0)
    lane = lax.broadcasted_iota(jnp.int32, shape, 1)
    pick = (dy == COLS * (lane // LANES) - lane % COLS).astype(F32).astype(BF16)
    fan_ref[...] = jnp.dot(taps_ref[...].astype(BF16), pick, preferred_element_type=F32)
    depth = turned_ref.shape[0]
    group = lane_group((depth, LANES))
    for e in range(3):
        lanes = slice(e * LANES, (e + 1) * LANES)
        turned = jnp.zeros((depth, LANES), F32)
        for r in range(ROWS):
            turned = jnp.where(group == r, fan_ref[ROWS - r : ROWS - r + depth, lanes], turned)
        turned_ref[:, lanes] = turned
    shape = (COLS, LANES)
    later = lax.broadcasted_iota(jnp.int32, shape, 1) % COLS >= lax.broadcasted_iota(
        jnp.int32, shape, 0
    )
    nothing = jnp.zeros((LANES, LANES), BF16)
    for e in range(3):
        bands_ref[0, e, :LANES, LANES:] = nothing
        bands_ref[2, e, LANES:, :LANES] = nothing
    for dq in range(depth // ROWS):
        for r in range(ROWS):
            at = dq * ROWS + r
            lines = [
                jnp.broadcast_to(turned_ref[at : at + 1, e * LANES : (e + 1) * LANES], shape)
                for e in range(3)
            ]
            same = [pltpu.roll(line, 0, 1, stride=1, stride_axis=0) for line in lines]
            next_ = [
                pltpu.roll(line, LANES - COLS, 1, stride=1, stride_axis=0) for line in lines[1:]
            ]
            next_.append(jnp.zeros(shape, F32))
            for e in range(3):
                block = jnp.where(later, same[e], next_[e]).astype(BF16)
                for a in range(2):
                    first = (dq + a) % 2 * LANES + r * COLS
                    bands_ref[
                        (dq + a) // 2, e, first : first + COLS, a * LANES : (a + 1) * LANES
                    ] = block


def render_all(raw_ref, bins_ref):
    blocks, groups = raw_ref.shape[:2]

    @pl.loop(0, blocks)
    def _(k):
        for q in range(groups):
            bins_ref[k, :, q * LANES : (q + 1) * LANES] = render(raw_ref[k, q])


def smoothed(bins_ref, bands_ref, t):
    blocks = bins_ref.shape[0]
    nothing = jnp.zeros(bins_ref.shape[1:], BF16)
    shifted_rows = []
    for e in range(3):
        parts = [bins_ref[k] for k in range(max(e - 1, 0), min(blocks + e - 1, blocks))]
        parts = [nothing] * (e == 0) + parts + [nothing] * (e == 2)
        shifted_rows.append(jnp.concatenate(parts, axis=0))
    right = bands_ref[t].reshape(3 * 2 * LANES, 2 * LANES)
    return jnp.dot(jnp.concatenate(shifted_rows, axis=1), right, preferred_element_type=F32)


def own_kernel(
    raw_ref,
    footprint_ref,
    gates_ref,
    total_ref,
    bands_ref,
    mix_ref,
    bins_ref,
    taps_ref,
    fan_ref,
    turned_ref,
    mixed_ref,
):
    render_all(raw_ref, bins_ref)
    weights(footprint_ref, taps_ref, fan_ref, turned_ref, bands_ref)
    gates, bins = gates_ref.shape
    half = mix_ref.shape[0] // 2
    mixed_ref[...] = jnp.zeros_like(mixed_ref)
    for s in range(2):
        mixed_ref[s * half : s * half + gates, s * bins : (s + 1) * bins] = gates_ref[...].astype(F32)
    mix_ref[...] = mixed_ref[...].astype(BF16)
    total_ref[...] = smoothed(bins_ref, bands_ref, 1)


def before_kernel(raw_ref, bands_ref, total_ref, more_ref, bins_ref):
    render_all(raw_ref, bins_ref)
    more_ref[...] = total_ref[...] + smoothed(bins_ref, bands_ref, 0)


def parity():
    return lax.rem(lax.axis_index("cross"), 2)


def edge_kernel(after_ref, raw_ref, before_ref, total_ref, outer_ref, inner_ref):
    groups = raw_ref.shape[1]
    end = raw_ref.shape[0] - 1
    for target, k in ((outer_ref, end * parity()), (inner_ref, end * (1 - parity()))):
        for at, source in enumerate((before_ref, raw_ref, after_ref)):
            target[at * groups : (at + 1) * groups] = source[k]


def after_kernel(raw_ref, bands_ref, mix_ref, total_ref, ends_ref, mid_ref, bins_ref):
    render_all(raw_ref, bins_ref)
    blocks, deep = bins_ref.shape[:2]
    total = total_ref[...] + smoothed(bins_ref, bands_ref, 2)
    ends_ref[0] = total[:deep]
    ends_ref[1] = total[(blocks - 1) * deep :]
    smooth = total[deep : (blocks - 1) * deep].astype(BF16)
    for k in range(blocks - 2):
        mid_ref[k] = jnp.dot(
            mix_ref[...], smooth[k * deep : (k + 1) * deep], preferred_element_type=F32
        )


def side_block(raw_ref, side, bands_ref, mix_ref, ends_ref):
    groups = raw_ref.shape[0] // 3
    left = jnp.concatenate([render(raw_ref[at]) for at in range(3 * groups)], axis=1)
    right = jnp.concatenate([bands_ref[t, 2 * side] for t in range(3)], axis=0)
    smooth = ends_ref[side] + jnp.dot(left, right, preferred_element_type=F32)
    return jnp.dot(mix_ref[...], smooth.astype(BF16), preferred_element_type=F32)


def finish_kernel(
    outer_ref, inner_ref, bands_ref, mix_ref, ends_ref, mid_ref, out_hbm, out_ref, sems
):
    groups = outer_ref.shape[0] // 3
    outer = side_block(outer_ref, parity(), bands_ref, mix_ref, ends_ref)
    inner = side_block(inner_ref, 1 - parity(), bands_ref, mix_ref, ends_ref)
    odd = parity() == 1
    mixed = [jnp.where(odd, inner, outer)]
    mixed += [mid_ref[k] for k in range(mid_ref.shape[0])]
    mixed += [jnp.where(odd, outer, inner)]
    half = mix_ref.shape[0] // 2
    rows = groups * ROWS
    gates = out_ref.shape[0] // (2 * rows)
    copies = []
    for s in range(2):
        for a in range(groups):
            for g in range(0, gates, 8):
                size = min(8, gates - g)
                parts = [
                    block[s * half + g : s * half + g + 8, a * LANES : (a + 1) * LANES]
                    for block in mixed
                ]
                for r, block in enumerate(swap_groups(parts)):
                    first = (s * gates + g) * rows + a * ROWS + r
                    out_ref[pl.ds(first, size, stride=rows), :] = block[:size]
        span = pl.ds(s * gates * rows, gates * rows)
        copies.append(pltpu.make_async_copy(out_ref.at[span], out_hbm.at[span], sems.at[s]))
        copies[-1].start()
    for copy in copies:
        copy.wait()


def vmem(*shape, dtype=BF16):
    return pltpu.VMEM(shape, dtype)


def far(*arrays):
    return [pltpu.with_memory_space_constraint(array, pltpu.HBM) for array in arrays]


def near(*arrays):
    return [pltpu.with_memory_space_constraint(array, pltpu.VMEM) for array in arrays]


def call(kernel, out, scratch, args, remote=(), place=pltpu.VMEM, alias=(), flops=0):
    whole = pl.BlockSpec(memory_space=pltpu.VMEM)
    there = pl.BlockSpec(memory_space=place)
    many = isinstance(out, (list, tuple))
    return pl.pallas_call(
        kernel,
        out_shape=out,
        in_specs=[whole] * len(args) + [pl.BlockSpec(memory_space=pl.ANY)] * len(remote),
        out_specs=[there] * len(out) if many else there,
        scratch_shapes=scratch,
        input_output_aliases=dict(alias),
        compiler_params=pltpu.CompilerParams(vmem_limit_bytes=LIMIT),
        cost_estimate=pl.CostEstimate(flops=flops, bytes_accessed=0, transcendentals=0),
    )(*near(*args), *far(*remote))


def shifted(array, axis, ahead):
    count = lax.axis_size(axis)
    pairs = [(i, i + 1) if ahead else (i + 1, i) for i in range(count - 1)]
    return lax.ppermute(array, axis, pairs)


def exchanged(array, axis, first):
    count = lax.axis_size(axis)
    pairs = [(i, i + 1) for i in range(first, count - 1, 2)]
    return lax.ppermute(array, axis, pairs + [(j, i) for i, j in pairs])


def local(interface_bins, layer_count, layer_values, footprint, depth_gate):
    samples, layers, rows, width = layer_values.shape
    gates = depth_gate.shape[1]
    blocks, groups, channels = width // COLS, rows // ROWS, 2 * layers * samples
    lines = -(-footprint.shape[0] // ROWS) * ROWS
    deep = samples * BINS

    raw, taps, turned = call(
        pack_kernel,
        [
            vmem(blocks, groups, channels, LANES),
            vmem(*footprint.shape),
            vmem(gates, BINS),
        ],
        [
            vmem(channels * rows, width, dtype=F32),
            vmem(*interface_bins.shape, dtype=jnp.int32),
            vmem(*layer_count.shape, dtype=jnp.int32),
            vmem(*layer_values.shape),
            pltpu.SemaphoreType.DMA((3 * samples + 2,)),
        ],
        (),
        remote=(interface_bins, layer_count, layer_values, footprint, depth_gate.T),
    )
    after = shifted(raw, "along", False)
    before = shifted(raw, "along", True)
    bins = vmem(blocks, deep, groups * LANES)
    sums = vmem(blocks * deep, groups * LANES, dtype=F32)
    total, bands, mix = call(
        own_kernel,
        [sums, vmem(3, 3, 2 * LANES, 2 * LANES), vmem(64, deep)],
        [
            bins,
            vmem(64, LANES, dtype=F32),
            vmem(64, 3 * LANES, dtype=F32),
            vmem(lines, 3 * LANES, dtype=F32),
            vmem(64, deep, dtype=F32),
        ],
        (raw, taps, turned),
        flops=2_000_000_000,
    )
    total = call(before_kernel, sums, [bins], (before, bands, total), alias={2: 0}, flops=10**9)
    outer, inner = call(
        edge_kernel,
        [vmem(3 * groups, channels, LANES)] * 2,
        [],
        (after, raw, before, total),
    )
    outer = exchanged(outer, "cross", 1)
    inner = exchanged(inner, "cross", 0)
    ends, mid = call(
        after_kernel,
        [
            vmem(2, deep, groups * LANES, dtype=F32),
            vmem(blocks - 2, 64, groups * LANES, dtype=F32),
        ],
        [bins],
        (after, bands, mix, total),
        flops=10**9,
    )
    out = call(
        finish_kernel,
        jax.ShapeDtypeStruct((samples * gates * rows, width), F32),
        [
            vmem(samples * gates * rows, width, dtype=F32),
            pltpu.SemaphoreType.DMA((samples,)),
        ],
        (outer, inner, bands, mix, ends, mid),
        place=pl.ANY,
    )
    return out.reshape(samples, gates, rows, width)


def solution(mesh):
    in_specs = (
        P(None, None, "along", "cross"),
        P(None, "along", "cross"),
        P(None, None, "along", "cross"),
        P(),
        P(),
    )
    out_specs = P(None, None, "along", "cross")
    return jax.shard_map(local, mesh=mesh, in_specs=in_specs, out_specs=out_specs, check_vma=False)
```

```python
import functools

import jax
import jax.numpy as jnp
from jax import lax
from jax.experimental import pallas as pl
from jax.experimental.pallas import tpu as pltpu
from jax.sharding import PartitionSpec as P

ROWS = 8
COLS = 16
LANES = 128
BINS = 64
LIMIT = 40 * 1024 * 1024
BF16 = jnp.bfloat16
F32 = jnp.float32

NETWORK = (
    (0, 6), (2, 3), (4, 5),
    (0, 2), (1, 4), (3, 6),
    (0, 1), (2, 5), (3, 4),
    (1, 2), (4, 6),
    (2, 3), (4, 5),
    (1, 2), (3, 4), (5, 6),
)


def lane_group(shape):
    return lax.broadcasted_iota(jnp.int32, shape, len(shape) - 1) // COLS


def staggered(parts, sign):
    count = len(parts)
    group = lane_group(parts[0].shape)
    step = 1
    while step < count:
        chosen = (group // step) % 2 == 1
        parts = [
            jnp.where(chosen, parts[(m + sign * step) % count], parts[m]) for m in range(count)
        ]
        step *= 2
    return parts


def swap_groups(parts):
    count = len(parts)
    parts = [
        pltpu.roll(part, COLS * d, 1) if d else part for d, part in enumerate(staggered(parts, 1))
    ]
    return staggered([parts[-m % count] for m in range(count)], -1)


def pack_kernel(
    bounds_hbm,
    count_hbm,
    values_hbm,
    footprint_hbm,
    gates_hbm,
    raw_ref,
    footprint_ref,
    gates_ref,
    plane_ref,
    bounds_ref,
    count_ref,
    values_ref,
    sems,
):
    samples, layers = values_ref.shape[:2]
    rows = count_ref.shape[1]
    channels = 2 * layers
    copies = []
    for s in range(samples):
        for source, target in (
            (bounds_hbm, bounds_ref), (count_hbm, count_ref), (values_hbm, values_ref)
        ):
            copies.append((source.at[s], target.at[s]))
    copies += [(footprint_hbm, footprint_ref), (gates_hbm, gates_ref)]
    copies = [
        pltpu.make_async_copy(source, target, sems.at[at])
        for at, (source, target) in enumerate(copies)
    ]
    for copy in copies:
        copy.start()
    for s in range(samples):
        for copy in copies[3 * s : 3 * s + 3]:
            copy.wait()
        count = count_ref[s]
        keys = [
            jnp.where(k < count - 1, bounds_ref[s, k], BINS).astype(F32) for k in range(layers - 1)
        ]
        for low, high in NETWORK:
            keys[low], keys[high] = (
                jnp.minimum(keys[low], keys[high]),
                jnp.maximum(keys[low], keys[high]),
            )
        planes = keys + [jnp.zeros_like(keys[0])]
        planes += [values_ref[s, k].astype(F32) for k in range(layers)]
        for k, plane in enumerate(planes):
            first = (s * channels + k) * rows
            plane_ref[first : first + rows, :] = plane
        for q in range(rows // ROWS):
            parts = []
            for r in range(ROWS):
                first = s * channels * rows + q * ROWS + r
                parts.append(plane_ref[pl.ds(first, channels, stride=rows), :])
            for k, block in enumerate(swap_groups(parts)):
                raw_ref[k, q, s * channels : (s + 1) * channels, :] = block.astype(BF16)
    for copy in copies[3 * samples :]:
        copy.wait()


def render(raw):
    channels = raw.shape[0] // 2
    layers = channels // 2
    level = lax.broadcasted_iota(jnp.int32, (BINS, LANES), 0).astype(F32).astype(BF16)
    wide = raw.astype(F32)
    both = []
    for s in range(2):

        def row(k):
            line = wide[s * channels + k : s * channels + k + 1, :]
            line = jnp.broadcast_to(line, (16, LANES)).astype(BF16)
            return jnp.concatenate([line] * (BINS // 16), axis=0)

        bins = row(layers)
        for k in range(layers - 1):
            bins = jnp.where(row(k) <= level, row(layers + 1 + k), bins)
        both.append(bins)
    return jnp.concatenate(both, axis=0)


def weights(footprint_ref, taps_ref, fan_ref, turned_ref, bands_ref):
    side = footprint_ref.shape[0]
    taps_ref[...] = jnp.zeros_like(taps_ref)
    taps_ref[ROWS : ROWS + side, :side] = footprint_ref[...].astype(F32)
    shape = (LANES, 3 * LANES)
    dy = lax.broadcasted_iota(jnp.int32, shape, 0)
    lane = lax.broadcasted_iota(jnp.int32, shape, 1)
    pick = (dy == COLS * (lane // LANES) - lane % COLS).astype(F32).astype(BF16)
    fan_ref[...] = jnp.dot(taps_ref[...].astype(BF16), pick, preferred_element_type=F32)
    depth = turned_ref.shape[0]
    group = lane_group((depth, LANES))
    for e in range(3):
        lanes = slice(e * LANES, (e + 1) * LANES)
        turned = jnp.zeros((depth, LANES), F32)
        for r in range(ROWS):
            turned = jnp.where(group == r, fan_ref[ROWS - r : ROWS - r + depth, lanes], turned)
        turned_ref[:, lanes] = turned
    shape = (COLS, LANES)
    later = lax.broadcasted_iota(jnp.int32, shape, 1) % COLS >= lax.broadcasted_iota(
        jnp.int32, shape, 0
    )
    nothing = jnp.zeros((LANES, LANES), BF16)
    for e in range(3):
        bands_ref[0, e, :LANES, LANES:] = nothing
        bands_ref[2, e, LANES:, :LANES] = nothing
    for dq in range(depth // ROWS):
        for r in range(ROWS):
            at = dq * ROWS + r
            lines = [
                jnp.broadcast_to(turned_ref[at : at + 1, e * LANES : (e + 1) * LANES], shape)
                for e in range(3)
            ]
            same = [pltpu.roll(line, 0, 1, stride=1, stride_axis=0) for line in lines]
            next_ = [
                pltpu.roll(line, LANES - COLS, 1, stride=1, stride_axis=0) for line in lines[1:]
            ]
            next_.append(jnp.zeros(shape, F32))
            for e in range(3):
                block = jnp.where(later, same[e], next_[e]).astype(BF16)
                for a in range(2):
                    first = (dq + a) % 2 * LANES + r * COLS
                    bands_ref[
                        (dq + a) // 2, e, first : first + COLS, a * LANES : (a + 1) * LANES
                    ] = block


def render_all(raw_ref, bins_ref):
    blocks, groups = raw_ref.shape[:2]

    @pl.loop(0, blocks)
    def _(k):
        for q in range(groups):
            bins_ref[k, :, q * LANES : (q + 1) * LANES] = render(raw_ref[k, q])


def smoothed(bins_ref, bands_ref, t):
    blocks = bins_ref.shape[0]
    nothing = jnp.zeros(bins_ref.shape[1:], BF16)
    shifted_rows = []
    for e in range(3):
        parts = [bins_ref[k] for k in range(max(e - 1, 0), min(blocks + e - 1, blocks))]
        parts = [nothing] * (e == 0) + parts + [nothing] * (e == 2)
        shifted_rows.append(jnp.concatenate(parts, axis=0))
    right = bands_ref[t].reshape(3 * 2 * LANES, 2 * LANES)
    return jnp.dot(jnp.concatenate(shifted_rows, axis=1), right, preferred_element_type=F32)


def own_kernel(
    raw_ref,
    footprint_ref,
    gates_ref,
    total_ref,
    bands_ref,
    mix_ref,
    bins_ref,
    taps_ref,
    fan_ref,
    turned_ref,
    mixed_ref,
):
    render_all(raw_ref, bins_ref)
    weights(footprint_ref, taps_ref, fan_ref, turned_ref, bands_ref)
    gates, bins = gates_ref.shape
    half = mix_ref.shape[0] // 2
    mixed_ref[...] = jnp.zeros_like(mixed_ref)
    for s in range(2):
        mixed_ref[s * half : s * half + gates, s * bins : (s + 1) * bins] = gates_ref[...].astype(F32)
    mix_ref[...] = mixed_ref[...].astype(BF16)
    total_ref[...] = smoothed(bins_ref, bands_ref, 1)


def odd_row():
    return lax.rem(lax.axis_index("along"), 2)


def parity():
    return lax.rem(lax.axis_index("cross"), 2)


def first_kernel(raw_ref, bands_ref, total_ref, more_ref, bins_ref):
    render_all(raw_ref, bins_ref)
    more_ref[...] = total_ref[...] + smoothed(bins_ref, bands_ref, 2 * (1 - odd_row()))


def edge_kernel(second_ref, raw_ref, late_ref, first_ref, total_ref, outer_ref, inner_ref):
    groups = raw_ref.shape[1]
    end = raw_ref.shape[0] - 1
    odd = odd_row() == 1
    for target, k in ((outer_ref, end * parity()), (inner_ref, end * (1 - parity()))):
        near_rows = first_ref[k] + late_ref[k]
        far_rows = second_ref[k]
        target[:groups] = jnp.where(odd, near_rows, far_rows)
        target[groups : 2 * groups] = raw_ref[k]
        target[2 * groups :] = jnp.where(odd, far_rows, near_rows)


def second_kernel(
    second_ref, late_ref, bands_ref, mix_ref, total_ref, ends_ref, mid_ref, bins_ref, sum_ref
):
    render_all(second_ref, bins_ref)
    blocks, deep = bins_ref.shape[:2]
    sum_ref[...] = total_ref[...] + smoothed(bins_ref, bands_ref, 2 * odd_row())

    @pl.when(is_late())
    def _():
        render_all(late_ref, bins_ref)
        sum_ref[...] += smoothed(bins_ref, bands_ref, 2 * (1 - odd_row()))

    ends_ref[0] = sum_ref[:deep]
    ends_ref[1] = sum_ref[(blocks - 1) * deep :]
    for k in range(blocks - 2):
        smooth = sum_ref[(k + 1) * deep : (k + 2) * deep].astype(BF16)
        mid_ref[k] = jnp.dot(mix_ref[...], smooth, preferred_element_type=F32)


def side_block(raw_ref, side, bands_ref, mix_ref, ends_ref):
    groups = raw_ref.shape[0] // 3
    left = jnp.concatenate([render(raw_ref[at]) for at in range(3 * groups)], axis=1)
    right = jnp.concatenate([bands_ref[t, 2 * side] for t in range(3)], axis=0)
    smooth = ends_ref[side] + jnp.dot(left, right, preferred_element_type=F32)
    return jnp.dot(mix_ref[...], smooth.astype(BF16), preferred_element_type=F32)


def finish_kernel(
    outer_ref, inner_ref, bands_ref, mix_ref, ends_ref, mid_ref, out_hbm, out_ref, sems
):
    groups = outer_ref.shape[0] // 3
    outer = side_block(outer_ref, parity(), bands_ref, mix_ref, ends_ref)
    inner = side_block(inner_ref, 1 - parity(), bands_ref, mix_ref, ends_ref)
    odd = parity() == 1
    mixed = [jnp.where(odd, inner, outer)]
    mixed += [mid_ref[k] for k in range(mid_ref.shape[0])]
    mixed += [jnp.where(odd, outer, inner)]
    half = mix_ref.shape[0] // 2
    rows = groups * ROWS
    gates = out_ref.shape[0] // (2 * rows)
    copies = []
    for s in range(2):
        for a in range(groups):
            for g in range(0, gates, 8):
                size = min(8, gates - g)
                parts = [
                    block[s * half + g : s * half + g + 8, a * LANES : (a + 1) * LANES]
                    for block in mixed
                ]
                for r, block in enumerate(swap_groups(parts)):
                    first = (s * gates + g) * rows + a * ROWS + r
                    out_ref[pl.ds(first, size, stride=rows), :] = block[:size]
        span = pl.ds(s * gates * rows, gates * rows)
        copies.append(pltpu.make_async_copy(out_ref.at[span], out_hbm.at[span], sems.at[s]))
        copies[-1].start()
    for copy in copies:
        copy.wait()


def vmem(*shape, dtype=BF16):
    return pltpu.VMEM(shape, dtype)


def far(*arrays):
    return [pltpu.with_memory_space_constraint(array, pltpu.HBM) for array in arrays]


def near(*arrays):
    return [pltpu.with_memory_space_constraint(array, pltpu.VMEM) for array in arrays]


def call(kernel, out, scratch, args, remote=(), place=pltpu.VMEM, alias=(), flops=0):
    whole = pl.BlockSpec(memory_space=pltpu.VMEM)
    there = pl.BlockSpec(memory_space=place)
    many = isinstance(out, (list, tuple))
    return pl.pallas_call(
        kernel,
        out_shape=out,
        in_specs=[whole] * len(args) + [pl.BlockSpec(memory_space=pl.ANY)] * len(remote),
        out_specs=[there] * len(out) if many else there,
        scratch_shapes=scratch,
        input_output_aliases=dict(alias),
        compiler_params=pltpu.CompilerParams(vmem_limit_bytes=LIMIT),
        cost_estimate=pl.CostEstimate(flops=flops, bytes_accessed=0, transcendentals=0),
    )(*near(*args), *far(*remote))


def late_pair(count):
    return (count // 2 - 2, count // 2 - 1) if count % 4 == 0 else None


def is_late():
    pair = late_pair(lax.axis_size("along"))
    here = lax.axis_index("along")
    return (here == pair[0]) | (here == pair[1]) if pair else here < 0


def swapped(array, axis, pairs):
    return lax.ppermute(array, axis, pairs + [(j, i) for i, j in pairs])


def pairs_from(first, count):
    return [(i, i + 1) for i in range(first, count - 1, 2)]


def local(interface_bins, layer_count, layer_values, footprint, depth_gate):
    samples, layers, rows, width = layer_values.shape
    gates = depth_gate.shape[1]
    blocks, groups, channels = width // COLS, rows // ROWS, 2 * layers * samples
    lines = -(-footprint.shape[0] // ROWS) * ROWS
    deep = samples * BINS

    raw, taps, turned = call(
        pack_kernel,
        [
            vmem(blocks, groups, channels, LANES),
            vmem(*footprint.shape),
            vmem(gates, BINS),
        ],
        [
            vmem(channels * rows, width, dtype=F32),
            vmem(*interface_bins.shape, dtype=jnp.int32),
            vmem(*layer_count.shape, dtype=jnp.int32),
            vmem(*layer_values.shape),
            pltpu.SemaphoreType.DMA((3 * samples + 2,)),
        ],
        (),
        remote=(interface_bins, layer_count, layer_values, footprint, depth_gate.T),
    )
    count = lax.axis_size("along")
    pair = late_pair(count)
    first = swapped(raw, "along", [p for p in pairs_from(0, count) if p != pair])
    second = swapped(raw, "along", pairs_from(1, count))
    late = swapped(raw, "along", [pair]) if pair else jnp.zeros_like(raw)
    bins = vmem(blocks, deep, groups * LANES)
    sums = vmem(blocks * deep, groups * LANES, dtype=F32)
    total, bands, mix = call(
        own_kernel,
        [sums, vmem(3, 3, 2 * LANES, 2 * LANES), vmem(64, deep)],
        [
            bins,
            vmem(64, LANES, dtype=F32),
            vmem(64, 3 * LANES, dtype=F32),
            vmem(lines, 3 * LANES, dtype=F32),
            vmem(64, deep, dtype=F32),
        ],
        (raw, taps, turned),
        flops=2_000_000_000,
    )
    total = call(first_kernel, sums, [bins], (first, bands, total), alias={2: 0}, flops=10**9)
    outer, inner = call(
        edge_kernel,
        [vmem(3 * groups, channels, LANES)] * 2,
        [],
        (second, raw, late, first, total),
    )
    wide = lax.axis_size("cross")
    outer = swapped(outer, "cross", pairs_from(1, wide))
    inner = swapped(inner, "cross", pairs_from(0, wide))
    ends, mid = call(
        second_kernel,
        [
            vmem(2, deep, groups * LANES, dtype=F32),
            vmem(blocks - 2, 64, groups * LANES, dtype=F32),
        ],
        [bins, sums],
        (second, late, bands, mix, total),
        flops=10**9,
    )
    out = call(
        finish_kernel,
        jax.ShapeDtypeStruct((samples * gates * rows, width), F32),
        [
            vmem(samples * gates * rows, width, dtype=F32),
            pltpu.SemaphoreType.DMA((samples,)),
        ],
        (outer, inner, bands, mix, ends, mid),
        place=pl.ANY,
    )
    return out.reshape(samples, gates, rows, width)


def solution(mesh):
    in_specs = (
        P(None, None, "along", "cross"),
        P(None, "along", "cross"),
        P(None, None, "along", "cross"),
        P(),
        P(),
    )
    out_specs = P(None, None, "along", "cross")
    return jax.shard_map(local, mesh=mesh, in_specs=in_specs, out_specs=out_specs, check_vma=False)
```

```python
import functools

import jax
import jax.numpy as jnp
from jax import lax
from jax.experimental import pallas as pl
from jax.experimental.pallas import tpu as pltpu
from jax.sharding import PartitionSpec as P

ROWS = 8
COLS = 16
LANES = 128
BINS = 64
LIMIT = 40 * 1024 * 1024
BF16 = jnp.bfloat16
F32 = jnp.float32

NETWORK = (
    (0, 6), (2, 3), (4, 5),
    (0, 2), (1, 4), (3, 6),
    (0, 1), (2, 5), (3, 4),
    (1, 2), (4, 6),
    (2, 3), (4, 5),
    (1, 2), (3, 4), (5, 6),
)


def lane_group(shape):
    return lax.broadcasted_iota(jnp.int32, shape, len(shape) - 1) // COLS


def staggered(parts, sign):
    count = len(parts)
    group = lane_group(parts[0].shape)
    step = 1
    while step < count:
        chosen = (group // step) % 2 == 1
        parts = [
            jnp.where(chosen, parts[(m + sign * step) % count], parts[m]) for m in range(count)
        ]
        step *= 2
    return parts


def swap_groups(parts):
    count = len(parts)
    parts = [
        pltpu.roll(part, COLS * d, 1) if d else part for d, part in enumerate(staggered(parts, 1))
    ]
    return staggered([parts[-m % count] for m in range(count)], -1)


def pack_kernel(
    bounds_hbm,
    count_hbm,
    values_hbm,
    footprint_hbm,
    gates_hbm,
    raw_ref,
    footprint_ref,
    gates_ref,
    plane_ref,
    bounds_ref,
    count_ref,
    values_ref,
    sems,
):
    samples, layers = values_ref.shape[:2]
    rows = count_ref.shape[1]
    channels = 2 * layers
    copies = []
    for s in range(samples):
        for source, target in (
            (bounds_hbm, bounds_ref), (count_hbm, count_ref), (values_hbm, values_ref)
        ):
            copies.append((source.at[s], target.at[s]))
    copies += [(footprint_hbm, footprint_ref), (gates_hbm, gates_ref)]
    copies = [
        pltpu.make_async_copy(source, target, sems.at[at])
        for at, (source, target) in enumerate(copies)
    ]
    for copy in copies:
        copy.start()
    for s in range(samples):
        for copy in copies[3 * s : 3 * s + 3]:
            copy.wait()
        count = count_ref[s]
        keys = [
            jnp.where(k < count - 1, bounds_ref[s, k], BINS).astype(F32) for k in range(layers - 1)
        ]
        for low, high in NETWORK:
            keys[low], keys[high] = (
                jnp.minimum(keys[low], keys[high]),
                jnp.maximum(keys[low], keys[high]),
            )
        planes = keys + [jnp.zeros_like(keys[0])]
        planes += [values_ref[s, k].astype(F32) for k in range(layers)]
        for k, plane in enumerate(planes):
            first = (s * channels + k) * rows
            plane_ref[first : first + rows, :] = plane
        for q in range(rows // ROWS):
            parts = []
            for r in range(ROWS):
                first = s * channels * rows + q * ROWS + r
                parts.append(plane_ref[pl.ds(first, channels, stride=rows), :])
            for k, block in enumerate(swap_groups(parts)):
                raw_ref[k, q, s * channels : (s + 1) * channels, :] = block.astype(BF16)
    for copy in copies[3 * samples :]:
        copy.wait()


def render(raw):
    channels = raw.shape[0] // 2
    layers = channels // 2
    level = lax.broadcasted_iota(jnp.int32, (BINS, LANES), 0).astype(F32).astype(BF16)
    wide = raw.astype(F32)
    both = []
    for s in range(2):

        def row(k):
            line = wide[s * channels + k : s * channels + k + 1, :]
            line = jnp.broadcast_to(line, (16, LANES)).astype(BF16)
            return jnp.concatenate([line] * (BINS // 16), axis=0)

        bins = row(layers)
        for k in range(layers - 1):
            bins = jnp.where(row(k) <= level, row(layers + 1 + k), bins)
        both.append(bins)
    return jnp.concatenate(both, axis=0)


def weights(footprint_ref, taps_ref, fan_ref, turned_ref, bands_ref):
    side = footprint_ref.shape[0]
    taps_ref[...] = jnp.zeros_like(taps_ref)
    taps_ref[ROWS : ROWS + side, :side] = footprint_ref[...].astype(F32)
    shape = (LANES, 3 * LANES)
    dy = lax.broadcasted_iota(jnp.int32, shape, 0)
    lane = lax.broadcasted_iota(jnp.int32, shape, 1)
    pick = (dy == COLS * (lane // LANES) - lane % COLS).astype(F32).astype(BF16)
    fan_ref[...] = jnp.dot(taps_ref[...].astype(BF16), pick, preferred_element_type=F32)
    depth = turned_ref.shape[0]
    group = lane_group((depth, LANES))
    for e in range(3):
        lanes = slice(e * LANES, (e + 1) * LANES)
        turned = jnp.zeros((depth, LANES), F32)
        for r in range(ROWS):
            turned = jnp.where(group == r, fan_ref[ROWS - r : ROWS - r + depth, lanes], turned)
        turned_ref[:, lanes] = turned
    shape = (COLS, LANES)
    later = lax.broadcasted_iota(jnp.int32, shape, 1) % COLS >= lax.broadcasted_iota(
        jnp.int32, shape, 0
    )
    nothing = jnp.zeros((LANES, LANES), BF16)
    for e in range(3):
        bands_ref[0, e, :LANES, LANES:] = nothing
        bands_ref[2, e, LANES:, :LANES] = nothing
    for dq in range(depth // ROWS):
        for r in range(ROWS):
            at = dq * ROWS + r
            lines = [
                jnp.broadcast_to(turned_ref[at : at + 1, e * LANES : (e + 1) * LANES], shape)
                for e in range(3)
            ]
            same = [pltpu.roll(line, 0, 1, stride=1, stride_axis=0) for line in lines]
            next_ = [
                pltpu.roll(line, LANES - COLS, 1, stride=1, stride_axis=0) for line in lines[1:]
            ]
            next_.append(jnp.zeros(shape, F32))
            for e in range(3):
                block = jnp.where(later, same[e], next_[e]).astype(BF16)
                for a in range(2):
                    first = (dq + a) % 2 * LANES + r * COLS
                    bands_ref[
                        (dq + a) // 2, e, first : first + COLS, a * LANES : (a + 1) * LANES
                    ] = block


def render_all(raw_ref, bins_ref):
    blocks, groups = raw_ref.shape[:2]

    @pl.loop(0, blocks)
    def _(k):
        for q in range(groups):
            bins_ref[k, :, q * LANES : (q + 1) * LANES] = render(raw_ref[k, q])


def smoothed(bins_ref, bands_ref, t):
    blocks = bins_ref.shape[0]
    nothing = jnp.zeros(bins_ref.shape[1:], BF16)
    shifted_rows = []
    for e in range(3):
        parts = [bins_ref[k] for k in range(max(e - 1, 0), min(blocks + e - 1, blocks))]
        parts = [nothing] * (e == 0) + parts + [nothing] * (e == 2)
        shifted_rows.append(jnp.concatenate(parts, axis=0))
    right = bands_ref[t].reshape(3 * 2 * LANES, 2 * LANES)
    return jnp.dot(jnp.concatenate(shifted_rows, axis=1), right, preferred_element_type=F32)


def own_kernel(
    raw_ref,
    footprint_ref,
    gates_ref,
    total_ref,
    bands_ref,
    mix_ref,
    bins_ref,
    taps_ref,
    fan_ref,
    turned_ref,
    mixed_ref,
):
    render_all(raw_ref, bins_ref)
    weights(footprint_ref, taps_ref, fan_ref, turned_ref, bands_ref)
    gates, bins = gates_ref.shape
    half = mix_ref.shape[0] // 2
    mixed_ref[...] = jnp.zeros_like(mixed_ref)
    for s in range(2):
        mixed_ref[s * half : s * half + gates, s * bins : (s + 1) * bins] = gates_ref[...].astype(F32)
    mix_ref[...] = mixed_ref[...].astype(BF16)
    total_ref[...] = smoothed(bins_ref, bands_ref, 1)


def odd_row():
    return lax.rem(lax.axis_index("along"), 2)


def parity():
    return lax.rem(lax.axis_index("cross"), 2)


def first_kernel(raw_ref, bands_ref, total_ref, more_ref, bins_ref):
    render_all(raw_ref, bins_ref)
    more_ref[...] = total_ref[...] + smoothed(bins_ref, bands_ref, 2 * (1 - odd_row()))


def edge_kernel(second_ref, raw_ref, late_ref, first_ref, total_ref, outer_ref, inner_ref):
    groups = raw_ref.shape[1]
    end = raw_ref.shape[0] - 1
    odd = odd_row() == 1
    for target, k in ((outer_ref, end * parity()), (inner_ref, end * (1 - parity()))):
        near_rows = first_ref[k] + late_ref[k]
        far_rows = second_ref[k]
        target[:groups] = jnp.where(odd, near_rows, far_rows)
        target[groups : 2 * groups] = raw_ref[k]
        target[2 * groups :] = jnp.where(odd, far_rows, near_rows)


def second_kernel(
    second_ref, late_ref, bands_ref, mix_ref, total_ref, ends_ref, mid_ref, bins_ref, sum_ref
):
    render_all(second_ref, bins_ref)
    blocks, deep = bins_ref.shape[:2]
    sum_ref[...] = total_ref[...] + smoothed(bins_ref, bands_ref, 2 * odd_row())

    @pl.when(is_late())
    def _():
        render_all(late_ref, bins_ref)
        sum_ref[...] += smoothed(bins_ref, bands_ref, 2 * (1 - odd_row()))

    ends_ref[0] = sum_ref[:deep]
    ends_ref[1] = sum_ref[(blocks - 1) * deep :]
    for k in range(blocks - 2):
        smooth = sum_ref[(k + 1) * deep : (k + 2) * deep].astype(BF16)
        mid_ref[k] = jnp.dot(mix_ref[...], smooth, preferred_element_type=F32)


def side_block(raw_ref, side, bands_ref, ends_ref):
    groups = raw_ref.shape[0] // 3
    left = jnp.concatenate([render(raw_ref[at]) for at in range(3 * groups)], axis=1)
    right = jnp.concatenate([bands_ref[t, 2 * side] for t in range(3)], axis=0)
    smooth = ends_ref[side] + jnp.dot(left, right, preferred_element_type=F32)
    return smooth.astype(BF16)


def finish_kernel(
    outer_ref, inner_ref, bands_ref, mix_ref, ends_ref, mid_ref, out_hbm, out_ref, sems
):
    groups = outer_ref.shape[0] // 3
    smooth = [
        side_block(outer_ref, parity(), bands_ref, ends_ref),
        side_block(inner_ref, 1 - parity(), bands_ref, ends_ref),
    ]
    both = jnp.dot(mix_ref[...], jnp.concatenate(smooth, axis=1), preferred_element_type=F32)
    outer, inner = both[:, : 2 * LANES], both[:, 2 * LANES :]
    odd = parity() == 1
    mixed = [jnp.where(odd, inner, outer)]
    mixed += [mid_ref[k] for k in range(mid_ref.shape[0])]
    mixed += [jnp.where(odd, outer, inner)]
    half = mix_ref.shape[0] // 2
    rows = groups * ROWS
    gates = out_ref.shape[0] // (2 * rows)
    copies = []
    for s in range(2):
        for a in range(groups):
            for g in range(0, gates, 8):
                size = min(8, gates - g)
                parts = [
                    block[s * half + g : s * half + g + 8, a * LANES : (a + 1) * LANES]
                    for block in mixed
                ]
                for r, block in enumerate(swap_groups(parts)):
                    first = (s * gates + g) * rows + a * ROWS + r
                    out_ref[pl.ds(first, size, stride=rows), :] = block[:size]
        span = pl.ds(s * gates * rows, gates * rows)
        copies.append(pltpu.make_async_copy(out_ref.at[span], out_hbm.at[span], sems.at[s]))
        copies[-1].start()
    for copy in copies:
        copy.wait()


def vmem(*shape, dtype=BF16):
    return pltpu.VMEM(shape, dtype)


def far(*arrays):
    return [pltpu.with_memory_space_constraint(array, pltpu.HBM) for array in arrays]


def near(*arrays):
    return [pltpu.with_memory_space_constraint(array, pltpu.VMEM) for array in arrays]


def call(kernel, out, scratch, args, remote=(), place=pltpu.VMEM, alias=(), flops=0):
    whole = pl.BlockSpec(memory_space=pltpu.VMEM)
    there = pl.BlockSpec(memory_space=place)
    many = isinstance(out, (list, tuple))
    return pl.pallas_call(
        kernel,
        out_shape=out,
        in_specs=[whole] * len(args) + [pl.BlockSpec(memory_space=pl.ANY)] * len(remote),
        out_specs=[there] * len(out) if many else there,
        scratch_shapes=scratch,
        input_output_aliases=dict(alias),
        compiler_params=pltpu.CompilerParams(vmem_limit_bytes=LIMIT),
        cost_estimate=pl.CostEstimate(flops=flops, bytes_accessed=0, transcendentals=0),
    )(*near(*args), *far(*remote))


def late_pair(count):
    return (count // 2 - 2, count // 2 - 1) if count % 4 == 0 else None


def is_late():
    pair = late_pair(lax.axis_size("along"))
    here = lax.axis_index("along")
    return (here == pair[0]) | (here == pair[1]) if pair else here < 0


def swapped(array, axis, pairs):
    return lax.ppermute(array, axis, pairs + [(j, i) for i, j in pairs])


def pairs_from(first, count):
    return [(i, i + 1) for i in range(first, count - 1, 2)]


def local(interface_bins, layer_count, layer_values, footprint, depth_gate):
    samples, layers, rows, width = layer_values.shape
    gates = depth_gate.shape[1]
    blocks, groups, channels = width // COLS, rows // ROWS, 2 * layers * samples
    lines = -(-footprint.shape[0] // ROWS) * ROWS
    deep = samples * BINS

    raw, taps, turned = call(
        pack_kernel,
        [
            vmem(blocks, groups, channels, LANES),
            vmem(*footprint.shape),
            vmem(gates, BINS),
        ],
        [
            vmem(channels * rows, width, dtype=F32),
            vmem(*interface_bins.shape, dtype=jnp.int32),
            vmem(*layer_count.shape, dtype=jnp.int32),
            vmem(*layer_values.shape),
            pltpu.SemaphoreType.DMA((3 * samples + 2,)),
        ],
        (),
        remote=(interface_bins, layer_count, layer_values, footprint, depth_gate.T),
    )
    count = lax.axis_size("along")
    pair = late_pair(count)
    first = swapped(raw, "along", [p for p in pairs_from(0, count) if p != pair])
    second = swapped(raw, "along", pairs_from(1, count))
    late = swapped(raw, "along", [pair]) if pair else jnp.zeros_like(raw)
    bins = vmem(blocks, deep, groups * LANES)
    sums = vmem(blocks * deep, groups * LANES, dtype=F32)
    total, bands, mix = call(
        own_kernel,
        [sums, vmem(3, 3, 2 * LANES, 2 * LANES), vmem(64, deep)],
        [
            bins,
            vmem(64, LANES, dtype=F32),
            vmem(64, 3 * LANES, dtype=F32),
            vmem(lines, 3 * LANES, dtype=F32),
            vmem(64, deep, dtype=F32),
        ],
        (raw, taps, turned),
        flops=2_000_000_000,
    )
    total = call(first_kernel, sums, [bins], (first, bands, total), alias={2: 0}, flops=10**9)
    outer, inner = call(
        edge_kernel,
        [vmem(3 * groups, channels, LANES)] * 2,
        [],
        (second, raw, late, first, total),
    )
    wide = lax.axis_size("cross")
    outer = swapped(outer, "cross", pairs_from(1, wide))
    inner = swapped(inner, "cross", pairs_from(0, wide))
    ends, mid = call(
        second_kernel,
        [
            vmem(2, deep, groups * LANES, dtype=F32),
            vmem(blocks - 2, 64, groups * LANES, dtype=F32),
        ],
        [bins, sums],
        (second, late, bands, mix, total),
        flops=10**9,
    )
    out = call(
        finish_kernel,
        jax.ShapeDtypeStruct((samples * gates * rows, width), F32),
        [
            vmem(samples * gates * rows, width, dtype=F32),
            pltpu.SemaphoreType.DMA((samples,)),
        ],
        (outer, inner, bands, mix, ends, mid),
        place=pl.ANY,
    )
    return out.reshape(samples, gates, rows, width)


def solution(mesh):
    in_specs = (
        P(None, None, "along", "cross"),
        P(None, "along", "cross"),
        P(None, None, "along", "cross"),
        P(),
        P(),
    )
    out_specs = P(None, None, "along", "cross")
    return jax.shard_map(local, mesh=mesh, in_specs=in_specs, out_specs=out_specs, check_vma=False)
```

```python
import functools

import jax
import jax.numpy as jnp
from jax import lax
from jax.experimental import pallas as pl
from jax.experimental.pallas import tpu as pltpu
from jax.sharding import PartitionSpec as P

ROWS = 8
COLS = 16
LANES = 128
BINS = 64
LIMIT = 40 * 1024 * 1024
BF16 = jnp.bfloat16
F32 = jnp.float32

NETWORK = (
    (0, 6), (2, 3), (4, 5),
    (0, 2), (1, 4), (3, 6),
    (0, 1), (2, 5), (3, 4),
    (1, 2), (4, 6),
    (2, 3), (4, 5),
    (1, 2), (3, 4), (5, 6),
)


def lane_group(shape):
    return lax.broadcasted_iota(jnp.int32, shape, len(shape) - 1) // COLS


def staggered(parts, sign):
    count = len(parts)
    group = lane_group(parts[0].shape)
    step = 1
    while step < count:
        chosen = (group // step) % 2 == 1
        parts = [
            jnp.where(chosen, parts[(m + sign * step) % count], parts[m]) for m in range(count)
        ]
        step *= 2
    return parts


def swap_groups(parts):
    count = len(parts)
    parts = [
        pltpu.roll(part, COLS * d, 1) if d else part for d, part in enumerate(staggered(parts, 1))
    ]
    return staggered([parts[-m % count] for m in range(count)], -1)


def pack_kernel(
    bounds_hbm,
    count_hbm,
    values_hbm,
    footprint_hbm,
    gates_hbm,
    raw_ref,
    footprint_ref,
    gates_ref,
    plane_ref,
    bounds_ref,
    count_ref,
    values_ref,
    sems,
):
    samples, layers = values_ref.shape[:2]
    rows = count_ref.shape[1]
    channels = 2 * layers
    copies = []
    for s in range(samples):
        for source, target in (
            (bounds_hbm, bounds_ref), (count_hbm, count_ref), (values_hbm, values_ref)
        ):
            copies.append((source.at[s], target.at[s]))
    copies += [(footprint_hbm, footprint_ref), (gates_hbm, gates_ref)]
    copies = [
        pltpu.make_async_copy(source, target, sems.at[at])
        for at, (source, target) in enumerate(copies)
    ]
    for copy in copies:
        copy.start()
    for s in range(samples):
        for copy in copies[3 * s : 3 * s + 3]:
            copy.wait()
        count = count_ref[s]
        keys = [
            jnp.where(k < count - 1, bounds_ref[s, k], BINS).astype(F32) for k in range(layers - 1)
        ]
        for low, high in NETWORK:
            keys[low], keys[high] = (
                jnp.minimum(keys[low], keys[high]),
                jnp.maximum(keys[low], keys[high]),
            )
        planes = keys + [jnp.zeros_like(keys[0])]
        planes += [values_ref[s, k].astype(F32) for k in range(layers)]
        for k, plane in enumerate(planes):
            first = (s * channels + k) * rows
            plane_ref[first : first + rows, :] = plane
        for q in range(rows // ROWS):
            parts = []
            for r in range(ROWS):
                first = s * channels * rows + q * ROWS + r
                parts.append(plane_ref[pl.ds(first, channels, stride=rows), :])
            for k, block in enumerate(swap_groups(parts)):
                raw_ref[k, q, s * channels : (s + 1) * channels, :] = block.astype(BF16)
    for copy in copies[3 * samples :]:
        copy.wait()


def render(raw):
    channels = raw.shape[0] // 2
    layers = channels // 2
    level = lax.broadcasted_iota(jnp.int32, (BINS, LANES), 0).astype(F32).astype(BF16)
    wide = raw.astype(F32)
    both = []
    for s in range(2):

        def row(k):
            line = wide[s * channels + k : s * channels + k + 1, :]
            line = jnp.broadcast_to(line, (16, LANES)).astype(BF16)
            return jnp.concatenate([line] * (BINS // 16), axis=0)

        bins = row(layers)
        for k in range(layers - 1):
            bins = jnp.where(row(k) <= level, row(layers + 1 + k), bins)
        both.append(bins)
    return jnp.concatenate(both, axis=0)


def weights(footprint_ref, taps_ref, fan_ref, turned_ref, bands_ref):
    side = footprint_ref.shape[0]
    taps_ref[...] = jnp.zeros_like(taps_ref)
    taps_ref[ROWS : ROWS + side, :side] = footprint_ref[...].astype(F32)
    shape = (LANES, 3 * LANES)
    dy = lax.broadcasted_iota(jnp.int32, shape, 0)
    lane = lax.broadcasted_iota(jnp.int32, shape, 1)
    pick = (dy == COLS * (lane // LANES) - lane % COLS).astype(F32).astype(BF16)
    fan_ref[...] = jnp.dot(taps_ref[...].astype(BF16), pick, preferred_element_type=F32)
    depth = turned_ref.shape[0]
    group = lane_group((depth, LANES))
    for e in range(3):
        lanes = slice(e * LANES, (e + 1) * LANES)
        turned = jnp.zeros((depth, LANES), F32)
        for r in range(ROWS):
            turned = jnp.where(group == r, fan_ref[ROWS - r : ROWS - r + depth, lanes], turned)
        turned_ref[:, lanes] = turned
    shape = (COLS, LANES)
    later = lax.broadcasted_iota(jnp.int32, shape, 1) % COLS >= lax.broadcasted_iota(
        jnp.int32, shape, 0
    )
    nothing = jnp.zeros((LANES, LANES), BF16)
    for e in range(3):
        bands_ref[0, e, :LANES, LANES:] = nothing
        bands_ref[2, e, LANES:, :LANES] = nothing
    for dq in range(depth // ROWS):
        for r in range(ROWS):
            at = dq * ROWS + r
            lines = [
                jnp.broadcast_to(turned_ref[at : at + 1, e * LANES : (e + 1) * LANES], shape)
                for e in range(3)
            ]
            same = [pltpu.roll(line, 0, 1, stride=1, stride_axis=0) for line in lines]
            next_ = [
                pltpu.roll(line, LANES - COLS, 1, stride=1, stride_axis=0) for line in lines[1:]
            ]
            next_.append(jnp.zeros(shape, F32))
            for e in range(3):
                block = jnp.where(later, same[e], next_[e]).astype(BF16)
                for a in range(2):
                    first = (dq + a) % 2 * LANES + r * COLS
                    bands_ref[
                        (dq + a) // 2, e, first : first + COLS, a * LANES : (a + 1) * LANES
                    ] = block


def render_all(raw_ref, bins_ref):
    blocks, groups = raw_ref.shape[:2]

    @pl.loop(0, blocks)
    def _(k):
        for q in range(groups):
            bins_ref[k, :, q * LANES : (q + 1) * LANES] = render(raw_ref[k, q])


def smoothed(bins_ref, bands_ref, t):
    blocks = bins_ref.shape[0]
    nothing = jnp.zeros(bins_ref.shape[1:], BF16)
    shifted_rows = []
    for e in range(3):
        parts = [bins_ref[k] for k in range(max(e - 1, 0), min(blocks + e - 1, blocks))]
        parts = [nothing] * (e == 0) + parts + [nothing] * (e == 2)
        shifted_rows.append(jnp.concatenate(parts, axis=0))
    right = bands_ref[t].reshape(3 * 2 * LANES, 2 * LANES)
    return jnp.dot(jnp.concatenate(shifted_rows, axis=1), right, preferred_element_type=F32)


def own_kernel(
    raw_ref,
    footprint_ref,
    gates_ref,
    total_ref,
    bands_ref,
    mix_ref,
    bins_ref,
    taps_ref,
    fan_ref,
    turned_ref,
    mixed_ref,
):
    render_all(raw_ref, bins_ref)
    weights(footprint_ref, taps_ref, fan_ref, turned_ref, bands_ref)
    gates, bins = gates_ref.shape
    half = mix_ref.shape[0] // 2
    mixed_ref[...] = jnp.zeros_like(mixed_ref)
    for s in range(2):
        mixed_ref[s * half : s * half + gates, s * bins : (s + 1) * bins] = gates_ref[...].astype(F32)
    mix_ref[...] = mixed_ref[...].astype(BF16)
    total_ref[...] = smoothed(bins_ref, bands_ref, 1)


def odd_row():
    return lax.rem(lax.axis_index("along"), 2)


def parity():
    return lax.rem(lax.axis_index("cross"), 2)


def first_kernel(raw_ref, bands_ref, total_ref, more_ref, bins_ref):
    render_all(raw_ref, bins_ref)
    more_ref[...] = total_ref[...] + smoothed(bins_ref, bands_ref, 2 * (1 - odd_row()))


def edge_kernel(second_ref, raw_ref, late_ref, first_ref, total_ref, outer_ref, inner_ref):
    groups = raw_ref.shape[1]
    end = raw_ref.shape[0] - 1
    odd = odd_row() == 1
    for target, k in ((outer_ref, end * parity()), (inner_ref, end * (1 - parity()))):
        near_rows = first_ref[k] + late_ref[k]
        far_rows = second_ref[k]
        target[:groups] = jnp.where(odd, near_rows, far_rows)
        target[groups : 2 * groups] = raw_ref[k]
        target[2 * groups :] = jnp.where(odd, far_rows, near_rows)


def second_kernel(
    second_ref, late_ref, bands_ref, mix_ref, total_ref, ends_ref, mid_ref, bins_ref, sum_ref
):
    render_all(second_ref, bins_ref)
    blocks, deep = bins_ref.shape[:2]
    sum_ref[...] = total_ref[...] + smoothed(bins_ref, bands_ref, 2 * odd_row())

    @pl.when(is_late())
    def _():
        render_all(late_ref, bins_ref)
        sum_ref[...] += smoothed(bins_ref, bands_ref, 2 * (1 - odd_row()))

    ends_ref[0] = sum_ref[:deep]
    ends_ref[1] = sum_ref[(blocks - 1) * deep :]
    for k in range(blocks - 2):
        smooth = sum_ref[(k + 1) * deep : (k + 2) * deep].astype(BF16)
        mid_ref[k] = jnp.dot(mix_ref[...], smooth, preferred_element_type=F32)


def side_block(raw_ref, side, bands_ref, ends_ref):
    groups = raw_ref.shape[0] // 3
    left = jnp.concatenate([render(raw_ref[at]) for at in range(3 * groups)], axis=1)
    right = jnp.concatenate([bands_ref[t, 2 * side] for t in range(3)], axis=0)
    smooth = ends_ref[side] + jnp.dot(left, right, preferred_element_type=F32)
    return smooth.astype(BF16)


def finish_kernel(
    outer_ref, inner_ref, bands_ref, mix_ref, ends_ref, mid_ref, out_hbm, out_ref, sems
):
    groups = outer_ref.shape[0] // 3
    odd = parity() == 1
    outer, inner = outer_ref[...], inner_ref[...]
    smooth = [
        side_block(jnp.where(odd, inner, outer), 0, bands_ref, ends_ref),
        side_block(jnp.where(odd, outer, inner), 1, bands_ref, ends_ref),
    ]
    both = jnp.dot(mix_ref[...], jnp.concatenate(smooth, axis=1), preferred_element_type=F32)
    mixed = [both[:, : 2 * LANES]]
    mixed += [mid_ref[k] for k in range(mid_ref.shape[0])]
    mixed += [both[:, 2 * LANES :]]
    half = mix_ref.shape[0] // 2
    rows = groups * ROWS
    gates = out_ref.shape[0] // (2 * rows)
    copies = []
    for s in range(2):
        for a in range(groups):
            for g in range(0, gates, 8):
                size = min(8, gates - g)
                parts = [
                    block[s * half + g : s * half + g + 8, a * LANES : (a + 1) * LANES]
                    for block in mixed
                ]
                for r, block in enumerate(swap_groups(parts)):
                    first = (s * gates + g) * rows + a * ROWS + r
                    out_ref[pl.ds(first, size, stride=rows), :] = block[:size]
        span = pl.ds(s * gates * rows, gates * rows)
        copies.append(pltpu.make_async_copy(out_ref.at[span], out_hbm.at[span], sems.at[s]))
        copies[-1].start()
    for copy in copies:
        copy.wait()


def vmem(*shape, dtype=BF16):
    return pltpu.VMEM(shape, dtype)


def far(*arrays):
    return [pltpu.with_memory_space_constraint(array, pltpu.HBM) for array in arrays]


def near(*arrays):
    return [pltpu.with_memory_space_constraint(array, pltpu.VMEM) for array in arrays]


def call(kernel, out, scratch, args, remote=(), place=pltpu.VMEM, alias=(), flops=0):
    whole = pl.BlockSpec(memory_space=pltpu.VMEM)
    there = pl.BlockSpec(memory_space=place)
    many = isinstance(out, (list, tuple))
    return pl.pallas_call(
        kernel,
        out_shape=out,
        in_specs=[whole] * len(args) + [pl.BlockSpec(memory_space=pl.ANY)] * len(remote),
        out_specs=[there] * len(out) if many else there,
        scratch_shapes=scratch,
        input_output_aliases=dict(alias),
        compiler_params=pltpu.CompilerParams(vmem_limit_bytes=LIMIT),
        cost_estimate=pl.CostEstimate(flops=flops, bytes_accessed=0, transcendentals=0),
    )(*near(*args), *far(*remote))


def late_pair(count):
    return (count // 2 - 2, count // 2 - 1) if count % 4 == 0 else None


def is_late():
    pair = late_pair(lax.axis_size("along"))
    here = lax.axis_index("along")
    return (here == pair[0]) | (here == pair[1]) if pair else here < 0


def swapped(array, axis, pairs):
    return lax.ppermute(array, axis, pairs + [(j, i) for i, j in pairs])


def pairs_from(first, count):
    return [(i, i + 1) for i in range(first, count - 1, 2)]


def local(interface_bins, layer_count, layer_values, footprint, depth_gate):
    samples, layers, rows, width = layer_values.shape
    gates = depth_gate.shape[1]
    blocks, groups, channels = width // COLS, rows // ROWS, 2 * layers * samples
    lines = -(-footprint.shape[0] // ROWS) * ROWS
    deep = samples * BINS

    raw, taps, turned = call(
        pack_kernel,
        [
            vmem(blocks, groups, channels, LANES),
            vmem(*footprint.shape),
            vmem(gates, BINS),
        ],
        [
            vmem(channels * rows, width, dtype=F32),
            vmem(*interface_bins.shape, dtype=jnp.int32),
            vmem(*layer_count.shape, dtype=jnp.int32),
            vmem(*layer_values.shape),
            pltpu.SemaphoreType.DMA((3 * samples + 2,)),
        ],
        (),
        remote=(interface_bins, layer_count, layer_values, footprint, depth_gate.T),
    )
    count = lax.axis_size("along")
    pair = late_pair(count)
    first = swapped(raw, "along", [p for p in pairs_from(0, count) if p != pair])
    second = swapped(raw, "along", pairs_from(1, count))
    late = swapped(raw, "along", [pair]) if pair else jnp.zeros_like(raw)
    bins = vmem(blocks, deep, groups * LANES)
    sums = vmem(blocks * deep, groups * LANES, dtype=F32)
    total, bands, mix = call(
        own_kernel,
        [sums, vmem(3, 3, 2 * LANES, 2 * LANES), vmem(64, deep)],
        [
            bins,
            vmem(64, LANES, dtype=F32),
            vmem(64, 3 * LANES, dtype=F32),
            vmem(lines, 3 * LANES, dtype=F32),
            vmem(64, deep, dtype=F32),
        ],
        (raw, taps, turned),
        flops=2_000_000_000,
    )
    total = call(first_kernel, sums, [bins], (first, bands, total), alias={2: 0}, flops=10**9)
    outer, inner = call(
        edge_kernel,
        [vmem(3 * groups, channels, LANES)] * 2,
        [],
        (second, raw, late, first, total),
    )
    wide = lax.axis_size("cross")
    outer = swapped(outer, "cross", pairs_from(1, wide))
    inner = swapped(inner, "cross", pairs_from(0, wide))
    ends, mid = call(
        second_kernel,
        [
            vmem(2, deep, groups * LANES, dtype=F32),
            vmem(blocks - 2, 64, groups * LANES, dtype=F32),
        ],
        [bins, sums],
        (second, late, bands, mix, total),
        flops=10**9,
    )
    out = call(
        finish_kernel,
        jax.ShapeDtypeStruct((samples * gates * rows, width), F32),
        [
            vmem(samples * gates * rows, width, dtype=F32),
            pltpu.SemaphoreType.DMA((samples,)),
        ],
        (outer, inner, bands, mix, ends, mid),
        place=pl.ANY,
    )
    return out.reshape(samples, gates, rows, width)


def solution(mesh):
    in_specs = (
        P(None, None, "along", "cross"),
        P(None, "along", "cross"),
        P(None, None, "along", "cross"),
        P(),
        P(),
    )
    out_specs = P(None, None, "along", "cross")
    return jax.shard_map(local, mesh=mesh, in_specs=in_specs, out_specs=out_specs, check_vma=False)
```
